128 devices in a mesh: inner: 32 (over y, z, core), rep: 4 (over x).
Axes of the slice: x: 4, y: 4, z: 4, core: 2. Of those that a mesh axis runs over, the one named last changes fastest.
Arguments:
- layer_input: bfloat16 [131072, 1024], P(('inner', 'rep')), may hold values from -6 to 6
- pre_act: bfloat16 [131072, 4096], P(('inner', 'rep')), may hold values from -5 to 5
- cotangent: bfloat16 [131072, 1024], P(('inner', 'rep')), may hold values from -1.25 to 1.25
- down_weight: bfloat16 [4096, 1024], replicated, may hold values from -0.09375 to 0.09375
- lengths: int32 [1024], P(('inner', 'rep')), may hold values from 32 to 128, as said below
Outputs:
- up_grad: float32 [1024, 4096], P('inner')
- down_grad: float32 [4096, 1024], P('inner')
The draws below stay inside these ranges and needn't reach their ends.
Inputs may be any that keep to these rules, and one draw needn't show every extreme that they name: `lengths`: some sequence is full and some has exactly 32 valid tokens in every draw; rows past a sequence's length are padding.
All inputs are finite; a program needn't handle non-finite values.
Results may differ from the reference program's by a relative error of at most 0.0013.
Values sent between devices are 32-bit elements; how exact they have to be, the bound alone decides.
No kernel may reach another device: no remote copies, remote signals or barrier semaphores. Data moves between devices by JAX's collectives and lax.ppermute only.
A program may use at most 192 MiB of HBM per device.

```python
import jax
import jax.numpy as jnp
from jax import lax

D = 1024
FF = 4096
SEQ = 128
SEQS_DEV = 8
LEVELS = 2
TOK_DEV = 1024
TOKENS = 131072
SEQS = 1024
N_INNER = 32
N_REP = 4


def draw_layer_input(key, part):
    key = jax.random.fold_in(key, 11)
    first_key, second_key = jax.random.split(key, 2)
    ramp = jnp.arange(D, dtype=jnp.float32) / (D - 1)
    rising = 0.05 + 0.95 * ramp
    common = jnp.clip(1.2 * jax.random.normal(first_key, (D,), jnp.float32), -2.0, 2.0)
    noise = jnp.clip(jax.random.normal(second_key, (TOKENS, D), jnp.float32), -4.0, 4.0)
    return ((rising * common)[None, :] + noise).astype(jnp.bfloat16)


def draw_pre_act(key, part):
    key = jax.random.fold_in(key, 14)
    ramp = jnp.arange(FF, dtype=jnp.float32) / (FF - 1)
    shift = -2.5 + 3.5 * ramp
    noise = jax.random.normal(key, (TOKENS, FF), jnp.float32)
    return jnp.clip(shift[None, :] + noise, -5.0, 5.0).astype(jnp.bfloat16)


def draw_cotangent(key, part):
    key = jax.random.fold_in(key, 12)
    first_key, second_key, third_key, fourth_key = jax.random.split(key, 4)
    position = jnp.arange(TOKENS, dtype=jnp.float32) / TOKENS
    rising = jnp.exp(jnp.log(3.0) * position)
    row_scale = jnp.exp(jax.random.uniform(third_key, (TOKENS,), jnp.float32, 0.0, jnp.log(10.0)))
    column_scale = jnp.exp(jax.random.uniform(fourth_key, (D,), jnp.float32, 0.0, jnp.log(10.0)))
    common = jnp.clip(0.02 * jax.random.normal(first_key, (D,), jnp.float32), -0.2, 0.2)
    noise = jnp.clip(jax.random.normal(second_key, (TOKENS, D), jnp.float32), -4.0, 4.0)
    values = (rising * row_scale)[:, None] * column_scale[None, :] * (common[None, :] + noise) / 1024.0
    return values.astype(jnp.bfloat16)


def draw_lengths(key, part):
    key = jax.random.fold_in(key, 13)
    drawn = jax.random.randint(key, (SEQS,), SEQ // 4, SEQ + 1, jnp.int32)
    drawn = drawn.at[0].set(SEQ)
    drawn = drawn.at[1].set(SEQ // 4)
    return drawn


def scatter_about(key, shape, spread, most, kind=jnp.bfloat16):
    result = spread * jax.random.normal(key, shape, jnp.float32)
    return jnp.clip(result, min=-most, max=most).astype(kind)


def setup_inputs(seed: int = 0) -> dict:
    seeds = jax.random.split(jax.random.key(seed), 6)
    layer_input = draw_layer_input(jax.random.fold_in(seeds[5], 71), 0)
    pre_act = draw_pre_act(jax.random.fold_in(seeds[5], 71), 0)
    cotangent = draw_cotangent(jax.random.fold_in(seeds[5], 71), 0)
    down_weight = scatter_about(seeds[3], (FF, D), FF ** -0.5, 0.09375)
    lengths = draw_lengths(jax.random.fold_in(seeds[5], 71), 0)
    return dict(layer_input=layer_input, pre_act=pre_act, cotangent=cotangent, down_weight=down_weight, lengths=lengths)


SQRT_HALF = 0.7071067811865476
INV_ROOT_TWO_PI = 0.3989422804014327
EPSILON = 1e-6


def block_grads(inputs, pre, cotan, weight, seq_lengths):
    row_count = inputs.shape[0]
    position = jnp.arange(row_count, dtype=jnp.int32)
    owner = position // SEQ
    allowed = seq_lengths[owner]
    is_valid = (position % SEQ) < allowed
    masked = jnp.where(is_valid[:, None], cotan, jnp.zeros_like(cotan))
    pre_wide = pre.astype(jnp.float32)
    cdf_value = 0.5 * (1.0 + jax.scipy.special.erf(pre_wide * SQRT_HALF))
    hidden = (pre_wide * cdf_value).astype(jnp.bfloat16)
    hidden_grad = lax.dot_general(masked, weight, (((1,), (1,)), ((), ())), preferred_element_type=jnp.float32)
    derivative = cdf_value + pre_wide * jnp.exp(-0.5 * pre_wide * pre_wide) * INV_ROOT_TWO_PI
    pre_grad = (hidden_grad * derivative).astype(jnp.bfloat16)
    up_block = lax.dot_general(inputs, pre_grad, (((0,), (0,)), ((), ())), preferred_element_type=jnp.float32)
    down_block = lax.dot_general(hidden, masked, (((0,), (0,)), ((), ())), preferred_element_type=jnp.float32)
    return up_block, down_block


def combine(first, second):
    cross = jnp.sum(first * second)
    first_coef = 1.0 - cross / (2.0 * (jnp.sum(first * first) + EPSILON))
    second_coef = 1.0 - cross / (2.0 * (jnp.sum(second * second) + EPSILON))
    return first_coef * first + second_coef * second


def reference(layer_input, pre_act, cotangent, down_weight, lengths):
    replicas = N_REP
    blocks = N_INNER * N_REP

    def accumulate(block, carry):
        up_acc, down_acc = carry
        row_start = (block * TOK_DEV).astype(jnp.int32)
        seq_start = (block * SEQS_DEV).astype(jnp.int32)
        inputs = lax.dynamic_slice_in_dim(layer_input, row_start, TOK_DEV, 0)
        pre = lax.dynamic_slice_in_dim(pre_act, row_start, TOK_DEV, 0)
        cotan = lax.dynamic_slice_in_dim(cotangent, row_start, TOK_DEV, 0)
        seq_lengths = lax.dynamic_slice_in_dim(lengths, seq_start, SEQS_DEV, 0)
        up_block, down_block = block_grads(inputs, pre, cotan, down_weight, seq_lengths)
        replica = (block % replicas).astype(jnp.int32)
        up_acc = up_acc.at[replica].add(up_block)
        down_acc = down_acc.at[replica].add(down_block)
        return up_acc, down_acc

    start_carry = (jnp.zeros((replicas, D, FF), jnp.float32), jnp.zeros((replicas, FF, D), jnp.float32))
    up_rep, down_rep = lax.fori_loop(0, blocks, accumulate, start_carry)
    vectors = [(up_rep[index], down_rep[index]) for index in range(replicas)]
    for level in range(LEVELS):
        half_count = len(vectors) // 2
        vectors = [(combine(vectors[index][0], vectors[index + half_count][0]),
                    combine(vectors[index][1], vectors[index + half_count][1])) for index in range(half_count)]
    return vectors[0][0], vectors[0][1]
```

```python
import jax
import jax.numpy as jnp
from jax import lax
from jax.sharding import PartitionSpec as P

SEQ = 128
RING = 4
CORES = 2


SQRT_HALF = 0.7071067811865476
INV_ROOT_TWO_PI = 0.3989422804014327
EPSILON = 1e-06


def device_of(y, z, core):
    return (y % RING * RING + z % RING) * CORES + core


def ring_route(stage, step):
    route = []
    for y in range(RING):
        for z in range(RING):
            for core in range(CORES):
                along_y = core == stage
                target = device_of(y + step, z, core) if along_y else device_of(y, z + step, core)
                route.append((device_of(y, z, core), target))
    return route


def core_route():
    return [(index, index ^ 1) for index in range(RING * RING * CORES)]


def axis_route(axis, step):
    route = []
    for y in range(RING):
        for z in range(RING):
            for core in range(CORES):
                target = device_of(y + step, z, core) if axis == 0 else device_of(y, z + step, core)
                route.append((device_of(y, z, core), target))
    return route


def inner_permute(block, route):
    return lax.ppermute(block, "inner", route)


def ring_reduce(pieces, stage):
    ahead, behind = ring_route(stage, 1), ring_route(stage, -1)
    from_behind = inner_permute(jnp.stack([pieces[2][0], pieces[1][1]]), ahead)
    from_ahead = inner_permute(jnp.stack([pieces[2][1], pieces[3][0]]), behind)
    first = inner_permute(pieces[1][0] + from_behind[0], ahead)
    second = inner_permute(pieces[3][1] + from_ahead[0], behind)
    return (
        pieces[0][0] + from_ahead[1] + first,
        pieces[0][1] + from_behind[1] + second,
    )


def reduce_group(keep, send):
    total = keep + inner_permute(send, core_route())
    once = ring_reduce([[total[k, h] for h in range(2)] for k in range(RING)], 0)
    twice = ring_reduce([[once[h][l] for h in range(2)] for l in range(RING)], 1)
    return jnp.concatenate(twice, axis=0)


def destinations(core_to):
    inner = lax.axis_index("inner")
    y, z = inner // (RING * CORES), inner // CORES % RING
    k = lax.iota(jnp.int32, RING)[:, None]
    l = lax.iota(jnp.int32, RING)[None, :]
    to_y = jnp.where(core_to == 0, y + k, y + l) % RING
    to_z = jnp.where(core_to == 0, z + l, z + k) % RING
    return (to_y * RING + to_z) * CORES + core_to


def arrange(grad, core_to):
    rows = grad.shape[0] // (RING * RING * CORES * 2)
    order = destinations(core_to)[:, None, :] * 2 + lax.iota(jnp.int32, 2)[None, :, None]
    return grad.reshape(-1, rows, grad.shape[1])[order]


def across_replicas(block):
    count = lax.axis_size("rep")
    replica = lax.axis_index("rep")
    held = [block]
    for step in range(1, count):
        held.append(lax.ppermute(block, "rep", [(i, (i - step) % count) for i in range(count)]))
    return [lax.select_n((index - replica) % count, *held) for index in range(count)]


def products(vectors):
    a, d, b, e = vectors
    terms = []
    for first, second in ((a, b), (d, e)):
        both = first + second
        terms += [first * first, second * second, first * second, both * both, both * (first - second)]
    terms += [a * d, a * e, b * d, b * e]
    return jnp.stack([jnp.sum(term) for term in terms])


def sum_inner(values):
    values = values + inner_permute(values, core_route())
    for axis in (0, 1):
        others = [inner_permute(values, axis_route(axis, step)) for step in (1, 2, 3)]
        values = (values + others[1]) + (others[0] + others[2])
    return values


def pair_coefs(first_sq, second_sq, cross, both_sq, difference):
    first_wide, second_wide = first_sq + EPSILON, second_sq + EPSILON
    first_coef = 1.0 - cross / (2.0 * first_wide)
    second_coef = 1.0 - cross / (2.0 * second_wide)
    plain = (first_coef * first_coef * first_sq + 2.0 * first_coef * second_coef * cross
             + second_coef * second_coef * second_sq)
    mean = 0.5 * (first_coef + second_coef)
    skew = 0.25 * (cross / first_wide) * (difference / second_wide)
    apart = first_sq + second_sq - 2.0 * cross
    opposite = mean * mean * both_sq + 2.0 * mean * skew * difference + skew * skew * apart
    square = jnp.where(both_sq < 0.25 * (first_sq + second_sq), opposite, plain)
    return first_coef, second_coef, square


def coefficients(t):
    a, b, left = pair_coefs(t[0], t[1], t[2], t[3], t[4])
    d, e, right = pair_coefs(t[5], t[6], t[7], t[8], t[9])
    cross = a * (d * t[10] + e * t[11]) + b * (d * t[12] + e * t[13])
    left_coef = 1.0 - cross / (2.0 * (left + EPSILON))
    right_coef = 1.0 - cross / (2.0 * (right + EPSILON))
    return left_coef * a, right_coef * d, left_coef * b, right_coef * e


def mix(vectors, coefs):
    a, d, b, e = [vector * coef for vector, coef in zip(vectors, coefs)]
    return (a + b) + (d + e)


def on_device(layer_input, pre_act, cotangent, down_weight, lengths):
    row_count = layer_input.shape[0]
    seq_count = lengths.shape[0]
    core = lax.axis_index("inner") % CORES
    position = lax.iota(jnp.int32, row_count)
    owner = position // SEQ
    belongs = owner[:, None] == lax.iota(jnp.int32, seq_count)[None, :]
    allowed = jnp.sum(jnp.where(belongs, lengths[None, :], 0), axis=1)
    is_valid = position % SEQ < allowed
    masked = jnp.where(is_valid[:, None], cotangent, jnp.zeros_like(cotangent))
    pre_wide = pre_act.astype(jnp.float32)
    cdf_value = 0.5 * (1.0 + jax.scipy.special.erf(pre_wide * SQRT_HALF))
    hidden = (pre_wide * cdf_value).astype(jnp.bfloat16)
    down = lax.dot_general(
        hidden, masked, (((0,), (0,)), ((), ())), preferred_element_type=jnp.float32
    )
    hidden_grad = lax.dot_general(
        masked, down_weight, (((1,), (1,)), ((), ())), preferred_element_type=jnp.float32
    )
    derivative = cdf_value + pre_wide * jnp.exp(-0.5 * pre_wide * pre_wide) * INV_ROOT_TWO_PI
    pre_grad = (hidden_grad * derivative).astype(jnp.bfloat16)
    up = lax.dot_general(
        layer_input, pre_grad, (((0,), (0,)), ((), ())), preferred_element_type=jnp.float32
    )
    outs = []
    for grad in (down, up):
        piece = reduce_group(arrange(grad, core), arrange(grad, 1 - core))
        vectors = across_replicas(piece)
        totals = sum_inner(products(vectors))
        outs.append(mix(vectors, coefficients(totals)))
    return (outs[1], outs[0])


def solution(mesh):
    in_specs = (
        P(("inner", "rep"), None),
        P(("inner", "rep"), None),
        P(("inner", "rep"), None),
        P(),
        P(("inner", "rep")),
    )
    out_specs = (P("inner", None), P("inner", None))
    return jax.shard_map(
        on_device, mesh=mesh, in_specs=in_specs, out_specs=out_specs, check_vma=False
    )
```

```python
import math

import jax
import jax.numpy as jnp
from jax import lax
from jax.experimental import pallas as pl
from jax.experimental.pallas import tpu as pltpu
from jax.sharding import PartitionSpec as P

SEQ = 128
RING = 4
CORES = 2
CHIPS = RING * RING
HALVES = 2
LANES = 128
FF_BLOCK = 256
UP_SPLITS = 2
MIB = 1024 * 1024

EPSILON = 1e-06
INV_ROOT_TWO_PI = 0.3989422804014327
EXP2_SCALE = -0.5 / math.log(2.0)
TAIL_SCALE = 0.28
TAIL = (0.11652077734470367, 0.06749676167964935, 0.26891013979911804,
        -0.2369934469461441, 0.38987401127815247, -0.10580823570489883)
TERMS = 14
TERM_ROWS = 16


def device_of(y, z, core):
    return (y % RING * RING + z % RING) * CORES + core


def inner_route(move):
    route = []
    for y in range(RING):
        for z in range(RING):
            for core in range(CORES):
                route.append((device_of(y, z, core), device_of(*move(y, z, core))))
    return route


def ring_route(stage, step):
    return inner_route(
        lambda y, z, core: (y + step, z, core) if core == stage else (y, z + step, core)
    )


def core_route():
    return inner_route(lambda y, z, core: (y, z, 1 - core))


def inner_permute(block, route):
    return lax.ppermute(block, "inner", route)


def ring_reduce(piece, stage):
    ahead, behind = ring_route(stage, 1), ring_route(stage, -1)
    from_behind = inner_permute(jnp.stack([piece(2, 0), piece(1, 1)]), ahead)
    from_ahead = inner_permute(jnp.stack([piece(2, 1), piece(3, 0)]), behind)
    first = inner_permute(piece(1, 0) + from_behind[0], ahead)
    second = inner_permute(piece(3, 1) + from_ahead[0], behind)
    return (
        lambda at: piece(0, 0)[at] + from_ahead[1][at] + first[at],
        lambda at: piece(0, 1)[at] + from_behind[1][at] + second[at],
    )


def reduce_group(keep, send):
    other = inner_permute(send, core_route())
    once = ring_reduce(lambda k, h: keep[k, h] + other[k, h], 0)
    twice = ring_reduce(lambda l, h: once[h](l), 1)
    return jnp.concatenate([half(slice(None)) for half in twice], axis=0)


def destination_table():
    inner = lax.axis_index("inner")
    y, z, core = inner // (RING * CORES), inner // CORES % RING, inner % CORES
    k = lax.iota(jnp.int32, RING)[:, None]
    l = lax.iota(jnp.int32, RING)[None, :]

    def order(core_to):
        to_y = jnp.where(core_to == 0, y + k, y + l) % RING
        to_z = jnp.where(core_to == 0, z + l, z + k) % RING
        return (to_y * RING + to_z) * CORES + core_to

    return jnp.stack([order(core), order(1 - core)])


def write_masked(lengths_ref, cotangent_ref, masked_ref):
    columns = cotangent_ref.shape[1]
    for seq in range(cotangent_ref.shape[0] // SEQ):
        rows = slice(seq * SEQ, (seq + 1) * SEQ)
        valid = lax.broadcasted_iota(jnp.int32, (SEQ, columns), 0) < lengths_ref[seq]
        values = cotangent_ref[rows, :].astype(jnp.float32)
        masked_ref[rows, :] = jnp.where(valid, values, 0.0).astype(masked_ref.dtype)


def up_kernel(rows_ref, lengths_ref, x_ref, cotangent_ref, pre_ref, weight_ref,
              keep_ref, send_ref, hidden_ref, turned_ref, ordered_ref, masked_ref, grad_ref):
    tokens, width = x_ref.shape
    strip = width // (CHIPS * CORES * HALVES)

    @pl.when(pl.program_id(0) == 0)
    def _():
        write_masked(lengths_ref, cotangent_ref, masked_ref)
        turned_ref[...] = x_ref[...].T
        for index in range(width // strip):
            start = pl.multiple_of(rows_ref[index], strip)
            ordered_ref[index * strip:(index + 1) * strip, :] = turned_ref[pl.ds(start, strip), :]

    part = tokens // 4
    for index in range(4):
        rows = slice(index * part, (index + 1) * part)
        hidden_grad = lax.dot_general(
            masked_ref[rows, :], weight_ref[...], (((1,), (1,)), ((), ())),
            preferred_element_type=jnp.float32,
        )
        value = pre_ref[rows, :].astype(jnp.float32)
        density = jnp.exp2(value * value * EXP2_SCALE)
        t = 1.0 / (1.0 + TAIL_SCALE * jnp.abs(value))
        poly = TAIL[-1]
        for term in TAIL[-2::-1]:
            poly = poly * t + term
        tail = poly * t * density
        cdf = jnp.where(value < 0.0, tail, 1.0 - tail)
        hidden_ref[rows, :] = (value * cdf).astype(hidden_ref.dtype)
        derivative = cdf + value * density * INV_ROOT_TWO_PI
        grad_ref[rows, :] = (hidden_grad * derivative).astype(grad_ref.dtype)
    half = width // CORES
    keep_ref[...] = jnp.dot(ordered_ref[:half, :], grad_ref[...], preferred_element_type=jnp.float32)
    send_ref[...] = jnp.dot(ordered_ref[half:, :], grad_ref[...], preferred_element_type=jnp.float32)


def up_call(table, lengths, x, cotangent, pre_act, weight, part):
    tokens, width = x.shape
    hidden_units = pre_act.shape[1] // UP_SPLITS
    steps = hidden_units // FF_BLOCK
    strip = width // (CHIPS * CORES * HALVES)
    half = lax.iota(jnp.int32, HALVES)[None, None, :, None]
    rows = (table[:, :, None, :] * HALVES + half).reshape(-1) * strip
    whole = pl.BlockSpec(memory_space=pltpu.VMEM)
    out_block = pl.BlockSpec((width // CORES, FF_BLOCK), lambda j, *_: (0, j))
    keep, send, hidden = pl.pallas_call(
        up_kernel,
        grid_spec=pltpu.PrefetchScalarGridSpec(
            num_scalar_prefetch=2,
            grid=(steps,),
            in_specs=[
                whole,
                whole,
                pl.BlockSpec((tokens, FF_BLOCK), lambda j, *_: (0, part * steps + j)),
                pl.BlockSpec((FF_BLOCK, width), lambda j, *_: (part * steps + j, 0)),
            ],
            out_specs=[
                out_block,
                out_block,
                pl.BlockSpec((tokens, FF_BLOCK), lambda j, *_: (0, j)),
            ],
            scratch_shapes=[
                pltpu.VMEM((width, tokens), jnp.bfloat16),
                pltpu.VMEM((width, tokens), jnp.bfloat16),
                pltpu.VMEM((tokens, width), jnp.bfloat16),
                pltpu.VMEM((tokens, FF_BLOCK), jnp.bfloat16),
            ],
        ),
        out_shape=[
            jax.ShapeDtypeStruct((width // CORES, hidden_units), jnp.float32),
            jax.ShapeDtypeStruct((width // CORES, hidden_units), jnp.float32),
            jax.ShapeDtypeStruct((tokens, hidden_units), jnp.bfloat16),
        ],
        compiler_params=pltpu.CompilerParams(vmem_limit_bytes=40 * MIB),
        cost_estimate=pl.CostEstimate(
            flops=4 * tokens * width * hidden_units,
            bytes_accessed=(4 * tokens * width + 4 * tokens * hidden_units
                            + 6 * width * hidden_units),
            transcendentals=2 * tokens * hidden_units,
        ),
        name="up_partial",
    )(rows, lengths, x, cotangent, pre_act, weight)
    shape = (RING, HALVES, RING, strip, hidden_units)
    return keep.reshape(shape), send.reshape(shape), hidden


def down_kernel(blocks_ref, lengths_ref, cotangent_ref, *refs):
    hidden_refs, (keep_ref, send_ref, masked_ref) = refs[:-3], refs[-3:]

    @pl.when(pl.program_id(0) == 0)
    def _():
        write_masked(lengths_ref, cotangent_ref, masked_ref)

    parts = len(hidden_refs) // 2
    index = pl.program_id(0)
    columns = []
    for which in range(2):
        block = blocks_ref[which * CHIPS + index]
        mine = hidden_refs[which * parts][...]
        for part in range(1, parts):
            other = hidden_refs[which * parts + part][...]
            count = CHIPS * CORES // parts
            mine = jnp.where(block // count == part, other, mine)
        columns.append(mine)
    product = lax.dot_general(
        jnp.concatenate(columns, axis=1), masked_ref[...], (((0,), (0,)), ((), ())),
        preferred_element_type=jnp.float32,
    )
    rows = product.shape[0] // 2
    keep_ref[...] = product[:rows].reshape(keep_ref.shape)
    send_ref[...] = product[rows:].reshape(send_ref.shape)


def down_call(table, lengths, cotangent, hidden_parts):
    tokens, width = cotangent.shape
    parts = len(hidden_parts)
    count = CHIPS * CORES // parts
    rows = hidden_parts[0].shape[1] // count
    blocks = table.reshape(-1)

    def hidden_spec(which, part):
        def place(i, blocks_ref, lengths_ref):
            block = blocks_ref[which * CHIPS + i] - part * count
            return 0, jnp.clip(block, 0, count - 1)

        return pl.BlockSpec((tokens, rows), place)

    out_block = pl.BlockSpec(
        (1, HALVES, 1, rows // HALVES, width), lambda i, *_: (i // RING, 0, i % RING, 0, 0)
    )
    out_shape = jax.ShapeDtypeStruct(
        (RING, HALVES, RING, rows // HALVES, width), jnp.float32
    )
    return pl.pallas_call(
        down_kernel,
        grid_spec=pltpu.PrefetchScalarGridSpec(
            num_scalar_prefetch=2,
            grid=(CHIPS,),
            in_specs=[pl.BlockSpec(memory_space=pltpu.VMEM)]
            + [hidden_spec(which, part) for which in range(2) for part in range(parts)],
            out_specs=[out_block, out_block],
            scratch_shapes=[pltpu.VMEM((tokens, width), jnp.bfloat16)],
        ),
        out_shape=[out_shape, out_shape],
        compiler_params=pltpu.CompilerParams(vmem_limit_bytes=40 * MIB),
        cost_estimate=pl.CostEstimate(
            flops=2 * tokens * width * rows * CHIPS * CORES,
            bytes_accessed=2 * tokens * width + (2 * tokens + 4 * width) * rows * CHIPS * CORES,
            transcendentals=0,
        ),
        name="down_partial",
    )(blocks, lengths, cotangent, *hidden_parts * 2)


def across_replicas(block):
    count = lax.axis_size("rep")
    held = [block]
    for step in range(1, count):
        held.append(lax.ppermute(block, "rep", [(i, (i - step) % count) for i in range(count)]))
    return held


def in_order(values, replica):
    once = [jnp.where(replica % 2 == 1, values[i - 1], values[i]) for i in range(4)]
    return [jnp.where(replica // 2 == 1, once[i - 2], once[i]) for i in range(4)]


def products_kernel(replica_ref, *refs):
    groups, out_ref = refs[:-1], refs[-1]
    replica = replica_ref[0]
    totals = jnp.zeros((TERMS * 8, LANES), jnp.float32)
    for first in range(0, len(groups), 4):
        held = groups[first:first + 4]
        rows, columns = held[0].shape

        def add_rows(index, totals):
            at = pl.ds(pl.multiple_of(index * 8, 8), 8)
            sums = [totals[i * 8:(i + 1) * 8, :] for i in range(TERMS)]
            for column in range(0, columns, LANES):
                values = [ref[at, column:column + LANES] for ref in held]
                a, d, b, e = in_order(values, replica)
                terms = []
                for left, right in ((a, b), (d, e)):
                    both = left + right
                    terms += [left * left, right * right, left * right, both * both,
                              both * (left - right)]
                terms += [a * d, a * e, b * d, b * e]
                sums = [total + term for total, term in zip(sums, terms)]
            return jnp.concatenate(sums, axis=0)

        totals = lax.fori_loop(0, rows // 8, add_rows, totals)
    for i in range(TERMS):
        out_ref[i:i + 1, :] = jnp.sum(totals[i * 8:(i + 1) * 8, :], axis=0, keepdims=True)
    out_ref[TERMS:, :] = jnp.zeros((TERM_ROWS - TERMS, LANES), jnp.float32)


def products_call(replica, groups):
    flat = [block for held in groups for block in held]
    vmem = pl.BlockSpec(memory_space=pltpu.VMEM)
    return pl.pallas_call(
        products_kernel,
        in_specs=[pl.BlockSpec(memory_space=pltpu.SMEM)] + [vmem] * len(flat),
        out_specs=vmem,
        out_shape=jax.ShapeDtypeStruct((TERM_ROWS, LANES), jnp.float32),
        compiler_params=pltpu.CompilerParams(vmem_limit_bytes=24 * MIB),
        cost_estimate=pl.CostEstimate(
            flops=TERMS * 2 * sum(block.size for block in flat) // 4,
            bytes_accessed=4 * sum(block.size for block in flat),
            transcendentals=0,
        ),
        name="inner_products",
    )(replica, *flat)


def sum_inner(values):
    values = values + inner_permute(values, core_route())
    for axis in (0, 1):
        others = [
            inner_permute(values, inner_route(
                lambda y, z, core: (y + step, z, core) if axis == 0 else (y, z + step, core)))
            for step in (1, 2, 3)
        ]
        values = (values + others[1]) + (others[0] + others[2])
    return values


def pair_coefs(first_sq, second_sq, cross, both_sq, difference):
    first_wide, second_wide = first_sq + EPSILON, second_sq + EPSILON
    first_coef = 1.0 - cross / (2.0 * first_wide)
    second_coef = 1.0 - cross / (2.0 * second_wide)
    plain = (first_coef * first_coef * first_sq + 2.0 * first_coef * second_coef * cross
             + second_coef * second_coef * second_sq)
    mean = 0.5 * (first_coef + second_coef)
    skew = 0.25 * (cross / first_wide) * (difference / second_wide)
    apart = first_sq + second_sq - 2.0 * cross
    opposite = mean * mean * both_sq + 2.0 * mean * skew * difference + skew * skew * apart
    square = jnp.where(both_sq < 0.25 * (first_sq + second_sq), opposite, plain)
    return first_coef, second_coef, square


def coefficients(t):
    a, b, left = pair_coefs(*t[0:5])
    d, e, right = pair_coefs(*t[5:10])
    cross = a * (d * t[10] + e * t[11]) + b * (d * t[12] + e * t[13])
    left_coef = 1.0 - cross / (2.0 * (left + EPSILON))
    right_coef = 1.0 - cross / (2.0 * (right + EPSILON))
    return left_coef * a, right_coef * d, left_coef * b, right_coef * e


def mix_kernel(replica_ref, totals_ref, *refs):
    groups, out_ref = refs[:-1], refs[-1]
    replica = replica_ref[0]
    totals = jnp.sum(totals_ref[...], axis=1, keepdims=True)
    coefs = coefficients([totals[i:i + 1, :] for i in range(TERMS)])
    start = 0
    for first in range(0, len(groups), 4):
        held = groups[first:first + 4]
        columns = held[0].shape[1]
        a, d, b, e = [
            value * coef for value, coef in zip(in_order([ref[...] for ref in held], replica), coefs)
        ]
        out_ref[:, start:start + columns] = (a + b) + (d + e)
        start += columns


def mix_call(replica, totals, groups):
    flat = [block for held in groups for block in held]
    rows = flat[0].shape[0]
    columns = sum(held[0].shape[1] for held in groups)
    vmem = pl.BlockSpec(memory_space=pltpu.VMEM)
    return pl.pallas_call(
        mix_kernel,
        in_specs=[pl.BlockSpec(memory_space=pltpu.SMEM)] + [vmem] * (len(flat) + 1),
        out_specs=vmem,
        out_shape=jax.ShapeDtypeStruct((rows, columns), jnp.float32),
        compiler_params=pltpu.CompilerParams(vmem_limit_bytes=24 * MIB),
        cost_estimate=pl.CostEstimate(
            flops=7 * rows * columns, bytes_accessed=20 * rows * columns, transcendentals=0
        ),
        name="combine",
    )(replica, totals, *flat)


def on_device(layer_input, pre_act, cotangent, down_weight, lengths):
    table = destination_table()
    replica = lax.axis_index("rep").reshape(1)
    up_groups, hidden_parts = [], []
    for part in range(UP_SPLITS):
        keep, send, hidden = up_call(
            table, lengths, layer_input, cotangent, pre_act, down_weight, part
        )
        up_groups.append(across_replicas(reduce_group(keep, send)))
        hidden_parts.append(hidden)
    keep, send = down_call(table, lengths, cotangent, hidden_parts)
    down_groups = [across_replicas(reduce_group(keep, send))]
    totals = sum_inner(jnp.stack([
        products_call(replica, up_groups), products_call(replica, down_groups)
    ]))
    return (
        mix_call(replica, totals[0], up_groups),
        mix_call(replica, totals[1], down_groups),
    )


def solution(mesh):
    in_specs = (
        P(("inner", "rep"), None),
        P(("inner", "rep"), None),
        P(("inner", "rep"), None),
        P(),
        P(("inner", "rep")),
    )
    out_specs = (P("inner", None), P("inner", None))
    return jax.shard_map(
        on_device, mesh=mesh, in_specs=in_specs, out_specs=out_specs, check_vma=False
    )
```

```python
import functools
import math

import jax
import jax.numpy as jnp
from jax import lax
from jax.experimental import pallas as pl
from jax.experimental.pallas import tpu as pltpu
from jax.sharding import PartitionSpec as P

SEQ = 128
RING = 4
CORES = 2
CHIPS = RING * RING
HALVES = 2
LANES = 128
FF_BLOCK = 512
MIB = 1024 * 1024

EPSILON = 1e-06
SQRT_HALF = 0.7071067811865476
INV_ROOT_TWO_PI = 0.3989422804014327
EXP2_SCALE = -0.5 / math.log(2.0)
TERMS = 14
TERM_ROWS = 16


def device_of(y, z, core):
    return (y % RING * RING + z % RING) * CORES + core


def inner_route(move):
    route = []
    for y in range(RING):
        for z in range(RING):
            for core in range(CORES):
                route.append((device_of(y, z, core), device_of(*move(y, z, core))))
    return route


def ring_route(stage, step):
    return inner_route(
        lambda y, z, core: (y + step, z, core) if core == stage else (y, z + step, core)
    )


def core_route():
    return inner_route(lambda y, z, core: (y, z, 1 - core))


def inner_permute(block, route):
    return lax.ppermute(block, "inner", route)


def ring_start(piece, stage):
    return (
        inner_permute(jnp.stack([piece(2, 0), piece(1, 1)]), ring_route(stage, 1)),
        inner_permute(jnp.stack([piece(2, 1), piece(3, 0)]), ring_route(stage, -1)),
    )


def ring_pass(piece, stage, received):
    from_behind, from_ahead = received
    return (
        inner_permute(piece(1, 0) + from_behind[0], ring_route(stage, 1)),
        inner_permute(piece(3, 1) + from_ahead[0], ring_route(stage, -1)),
    )


def ring_end(piece, received, passed):
    from_behind, from_ahead = received
    return (
        lambda at: piece(0, 0)[at] + from_ahead[1][at] + passed[0][at],
        lambda at: piece(0, 1)[at] + from_behind[1][at] + passed[1][at],
    )


def once_reduced(halves):
    return lambda l, h: halves[h](l)


def joined(halves):
    return jnp.concatenate([half(...) for half in halves], axis=-2)


def direct(halves):
    return [
        inner_permute(jnp.stack([half(step) for half in halves]), ring_route(1, step))
        for step in range(1, RING)
    ]


def direct_end(halves, received):
    one, two, three = received
    return jnp.concatenate(
        [(half(0) + two[h]) + (one[h] + three[h]) for h, half in enumerate(halves)], axis=-2
    )


def core_sum(keep, other):
    return lambda k, h: keep[k, h] + other[k, h]


def gate(arrived, earlier=()):
    return lax.optimization_barrier((arrived, earlier))[0]


def destination_table():
    inner = lax.axis_index("inner")
    y, z, core = inner // (RING * CORES), inner // CORES % RING, inner % CORES
    k = lax.iota(jnp.int32, RING)[:, None]
    l = lax.iota(jnp.int32, RING)[None, :]

    def order(core_to):
        to_y = jnp.where(core_to == 0, y + k, y + l) % RING
        to_z = jnp.where(core_to == 0, z + l, z + k) % RING
        return (to_y * RING + to_z) * CORES + core_to

    return jnp.stack([order(core), order(1 - core)])


def write_masked(lengths_ref, cotangent_ref, masked_ref):
    columns = cotangent_ref.shape[1]
    for seq in range(cotangent_ref.shape[0] // SEQ):
        rows = slice(seq * SEQ, (seq + 1) * SEQ)
        valid = lax.broadcasted_iota(jnp.int32, (SEQ, columns), 0) < lengths_ref[seq]
        values = cotangent_ref[rows, :].astype(jnp.float32)
        masked_ref[rows, :] = jnp.where(valid, values, 0.0).astype(masked_ref.dtype)


def prepare(rows_ref, lengths_ref, x_ref, cotangent_ref, ordered_ref, masked_ref, turned_ref):
    strip = x_ref.shape[1] // (CHIPS * CORES * HALVES)
    write_masked(lengths_ref, cotangent_ref, masked_ref)
    turned_ref[...] = x_ref[...].T
    for index in range(x_ref.shape[1] // strip):
        start = pl.multiple_of(rows_ref[index], strip)
        ordered_ref[index * strip:(index + 1) * strip, :] = turned_ref[pl.ds(start, strip), :]


def down_blocks(pre_refs, masked_ref, keep_ref, send_ref):
    rows = pre_refs[0].shape[1]
    for first in range(0, len(pre_refs), 2):
        columns = []
        for ref in pre_refs[first:first + 2]:
            value = ref[...].astype(jnp.float32)
            cdf = 0.5 + 0.5 * lax.erf(value * SQRT_HALF)
            columns.append((value * cdf).astype(jnp.bfloat16))
        product = lax.dot_general(
            jnp.concatenate(columns, axis=1), masked_ref[...], (((0,), (0,)), ((), ())),
            preferred_element_type=jnp.float32,
        )
        for index in range(2):
            which, place = divmod(first + index, len(pre_refs) // 2)
            out_ref = (keep_ref, send_ref)[which]
            part = product[index * rows:(index + 1) * rows]
            out_ref[0, :, place, :, :] = part.reshape(HALVES, rows // HALVES, part.shape[1])


def first_down_kernel(blocks_ref, rows_ref, lengths_ref, x_ref, cotangent_ref, *refs):
    pre_refs, (keep_ref, send_ref, ordered_ref, masked_ref, turned_ref) = refs[:-5], refs[-5:]

    @pl.when(pl.program_id(0) == 0)
    def _():
        prepare(rows_ref, lengths_ref, x_ref, cotangent_ref, ordered_ref, masked_ref, turned_ref)

    down_blocks(pre_refs, masked_ref, keep_ref, send_ref)


def down_kernel(blocks_ref, masked_ref, *refs):
    down_blocks(refs[:-2], masked_ref, *refs[-2:])


def down_call(table, pre_act, places, lengths=None, x=None, cotangent=None, masked=None):
    is_first = masked is None
    tokens, width = (cotangent if is_first else masked).shape
    rows = pre_act.shape[1] // (CHIPS * CORES)
    strip = width // (CHIPS * CORES * HALVES)

    def pre_spec(which, place):
        return pl.BlockSpec(
            (tokens, rows), lambda k, blocks_ref, *_: (0, blocks_ref[which * CHIPS + k * RING + place])
        )

    whole = pl.BlockSpec((tokens, width), lambda k, *_: (0, 0))
    turned = pl.BlockSpec((width, tokens), lambda k, *_: (0, 0))
    out_block = pl.BlockSpec(
        (1, HALVES, len(places), rows // HALVES, width), lambda k, *_: (k, 0, 0, 0, 0)
    )
    out_shape = [
        jax.ShapeDtypeStruct((RING, HALVES, len(places), rows // HALVES, width), jnp.float32)
    ] * 2
    prefetch, wholes, scratch, extra = [table.reshape(-1)], [masked], [], []
    if is_first:
        half = lax.iota(jnp.int32, HALVES)[None, None, :, None]
        strips = (table[:, :, None, :] * HALVES + half).reshape(-1) * strip
        prefetch, wholes = prefetch + [strips, lengths], [x, cotangent]
        scratch, extra = [pltpu.VMEM((width, tokens), jnp.bfloat16)], [turned, whole]
        out_shape = out_shape + [
            jax.ShapeDtypeStruct((width, tokens), jnp.bfloat16),
            jax.ShapeDtypeStruct((tokens, width), jnp.bfloat16),
        ]
    count = 2 * len(places)
    return pl.pallas_call(
        first_down_kernel if is_first else down_kernel,
        grid_spec=pltpu.PrefetchScalarGridSpec(
            num_scalar_prefetch=len(prefetch),
            grid=(RING,),
            in_specs=[whole] * len(wholes)
            + [pre_spec(which, place) for which in range(2) for place in places],
            out_specs=[out_block, out_block] + extra,
            scratch_shapes=scratch,
        ),
        out_shape=out_shape,
        compiler_params=pltpu.CompilerParams(vmem_limit_bytes=60 * MIB),
        cost_estimate=pl.CostEstimate(
            flops=2 * tokens * width * rows * RING * count,
            bytes_accessed=4 * tokens * width + (2 * tokens + 4 * width) * rows * RING * count,
            transcendentals=0,
        ),
        name="down_partial",
    )(*prefetch, *wholes, *[pre_act] * count)


def up_kernel(ordered_ref, masked_ref, pre_ref, weight_ref, *refs):
    keep_ref, send_ref = refs[-2:]
    tokens, width = masked_ref.shape
    grads = []
    part = tokens // 4
    for first in range(0, tokens, part):
        rows = slice(first, first + part)
        hidden_grad = lax.dot_general(
            masked_ref[rows, :], weight_ref[...], (((1,), (1,)), ((), ())),
            preferred_element_type=jnp.float32,
        )
        value = pre_ref[rows, :].astype(jnp.float32)
        cdf = 0.5 + 0.5 * lax.erf(value * SQRT_HALF)
        density = jnp.exp2(value * value * EXP2_SCALE)
        derivative = cdf + value * density * INV_ROOT_TWO_PI
        grads.append((hidden_grad * derivative).astype(jnp.bfloat16))
    grad = jnp.concatenate(grads, axis=0)
    half = width // CORES
    keep_ref[...] = jnp.dot(ordered_ref[:half, :], grad, preferred_element_type=jnp.float32)
    send_ref[...] = jnp.dot(ordered_ref[half:, :], grad, preferred_element_type=jnp.float32)


def up_call(ordered, masked, pre_act, weight, start, count):
    width, tokens = ordered.shape
    at = start // FF_BLOCK
    out_block = pl.BlockSpec((width // CORES, FF_BLOCK), lambda j: (0, j))
    out_shape = jax.ShapeDtypeStruct((width // CORES, count), jnp.float32)
    keep, send = pl.pallas_call(
        up_kernel,
        grid=(count // FF_BLOCK,),
        in_specs=[
            pl.BlockSpec((width, tokens), lambda j: (0, 0)),
            pl.BlockSpec((tokens, width), lambda j: (0, 0)),
            pl.BlockSpec((tokens, FF_BLOCK), lambda j: (0, at + j)),
            pl.BlockSpec((FF_BLOCK, width), lambda j: (at + j, 0)),
        ],
        out_specs=[out_block, out_block],
        out_shape=[out_shape, out_shape],
        compiler_params=pltpu.CompilerParams(vmem_limit_bytes=40 * MIB),
        cost_estimate=pl.CostEstimate(
            flops=4 * tokens * width * count,
            bytes_accessed=4 * tokens * width + 2 * tokens * count + 6 * width * count,
            transcendentals=2 * tokens * count,
        ),
        name="up_partial",
    )(ordered, masked, pre_act, weight)
    shape = (RING, HALVES, RING, width // (CHIPS * CORES * HALVES), count)
    return keep.reshape(shape), send.reshape(shape)


def replica_route(step):
    count = lax.axis_size("rep")
    return [(i, (i + step) % count) for i in range(count)]


def neighbours(block):
    return tuple(lax.ppermute(block, "rep", replica_route(step)) for step in (1, -1))


def opposite(received):
    from_behind, from_ahead = received
    half = from_behind.shape[0] // 2
    return (
        lax.ppermute(from_behind[:half], "rep", replica_route(1)),
        lax.ppermute(from_ahead[half:], "rep", replica_route(-1)),
    )


def held_blocks(block, received, far):
    return [block, received[1], jnp.concatenate(far, axis=0), received[0]]


def across_replicas(block):
    return [block] + [lax.ppermute(block, "rep", replica_route(-step)) for step in range(1, RING)]


def in_order(values, replica):
    once = [jnp.where(replica % 2 == 1, values[i - 1], values[i]) for i in range(4)]
    return [jnp.where(replica // 2 == 1, once[i - 2], once[i]) for i in range(4)]


def products_kernel(replica_ref, *refs):
    held, out_ref = refs[:-1], refs[-1]
    replica = replica_ref[0]
    rows, columns = held[0].shape[-2:]

    def add_rows(index, totals):
        at = pl.ds(pl.multiple_of(index * 8, 8), 8)
        sums = [totals[i * 8:(i + 1) * 8, :] for i in range(TERMS)]
        for column in range(0, columns, LANES):
            a, d, b, e = in_order(
                [ref[at, column:column + LANES] for ref in held], replica
            )
            terms = []
            for left, right in ((a, b), (d, e)):
                both = left + right
                terms += [left * left, right * right, left * right, both * both,
                          both * (left - right)]
            terms += [a * d, a * e, b * d, b * e]
            sums = [total + term for total, term in zip(sums, terms)]
        return jnp.concatenate(sums, axis=0)

    totals = lax.fori_loop(0, rows // 8, add_rows, jnp.zeros((TERMS * 8, LANES), jnp.float32))
    for i in range(TERMS):
        out_ref[i:i + 1, :] = jnp.sum(totals[i * 8:(i + 1) * 8, :], axis=0, keepdims=True)
    out_ref[TERMS:, :] = jnp.zeros((TERM_ROWS - TERMS, LANES), jnp.float32)


def products_call(replica, held):
    vmem = pl.BlockSpec(memory_space=pltpu.VMEM)
    return pl.pallas_call(
        products_kernel,
        in_specs=[pl.BlockSpec(memory_space=pltpu.SMEM)] + [vmem] * len(held),
        out_specs=vmem,
        out_shape=jax.ShapeDtypeStruct((TERM_ROWS, LANES), jnp.float32),
        compiler_params=pltpu.CompilerParams(vmem_limit_bytes=24 * MIB),
        cost_estimate=pl.CostEstimate(
            flops=TERMS * 2 * held[0].size, bytes_accessed=16 * held[0].size, transcendentals=0
        ),
        name="inner_products",
    )(replica, *held)


def sum_inner(values):
    values = values + inner_permute(values, core_route())
    for axis in (0, 1):
        others = [
            inner_permute(values, inner_route(
                lambda y, z, core: (y + step, z, core) if axis == 0 else (y, z + step, core)))
            for step in (1, 2, 3)
        ]
        values = (values + others[1]) + (others[0] + others[2])
    return values


def pair_coefs(first_sq, second_sq, cross, both_sq, difference):
    first_wide, second_wide = first_sq + EPSILON, second_sq + EPSILON
    first_coef = 1.0 - cross / (2.0 * first_wide)
    second_coef = 1.0 - cross / (2.0 * second_wide)
    plain = (first_coef * first_coef * first_sq + 2.0 * first_coef * second_coef * cross
             + second_coef * second_coef * second_sq)
    mean = 0.5 * (first_coef + second_coef)
    skew = 0.25 * (cross / first_wide) * (difference / second_wide)
    apart = first_sq + second_sq - 2.0 * cross
    opposite = mean * mean * both_sq + 2.0 * mean * skew * difference + skew * skew * apart
    square = jnp.where(both_sq < 0.25 * (first_sq + second_sq), opposite, plain)
    return first_coef, second_coef, square


def coefficients(t):
    a, b, left = pair_coefs(*t[0:5])
    d, e, right = pair_coefs(*t[5:10])
    cross = a * (d * t[10] + e * t[11]) + b * (d * t[12] + e * t[13])
    left_coef = 1.0 - cross / (2.0 * (left + EPSILON))
    right_coef = 1.0 - cross / (2.0 * (right + EPSILON))
    return left_coef * a, right_coef * d, left_coef * b, right_coef * e


def mix_kernel(counts, replica_ref, totals_ref, *refs):
    groups, outs = refs[:-len(counts)], refs[-len(counts):]
    replica = replica_ref[0]
    group = 0
    for count, out_ref in zip(counts, outs):
        totals = totals_ref[group]
        for index in range(1, count):
            totals = totals + totals_ref[group + index]
        totals = jnp.sum(totals, axis=1, keepdims=True)
        coefs = coefficients([totals[i:i + 1, :] for i in range(TERMS)])
        start = 0
        for index in range(group, group + count):
            held = groups[4 * index:4 * index + 4]
            rows, columns = out_ref.shape[0], held[0].shape[1]
            for first in range(0, held[0].shape[0], rows):
                values = in_order([ref[first:first + rows, :] for ref in held], replica)
                a, d, b, e = [value * coef for value, coef in zip(values, coefs)]
                out_ref[:, start:start + columns] = (a + b) + (d + e)
                start += columns
        group += count


def mix_call(replica, totals, rows, outs):
    vmem = pl.BlockSpec(memory_space=pltpu.VMEM)
    flat = [block for groups in outs for held in groups for block in held]
    shapes = [
        jax.ShapeDtypeStruct((count, sum(held[0].size for held in groups) // count), jnp.float32)
        for count, groups in zip(rows, outs)
    ]
    size = sum(shape.size for shape in shapes)
    return pl.pallas_call(
        functools.partial(mix_kernel, [len(groups) for groups in outs]),
        in_specs=[pl.BlockSpec(memory_space=pltpu.SMEM)] + [vmem] * (len(flat) + 1),
        out_specs=[vmem] * len(shapes),
        out_shape=shapes,
        compiler_params=pltpu.CompilerParams(vmem_limit_bytes=24 * MIB),
        cost_estimate=pl.CostEstimate(flops=7 * size, bytes_accessed=20 * size, transcendentals=0),
        name="combine",
    )(replica, totals, *flat)


ORDER = ['d0', 'd1', 'e0', 'e1', 'a0', 'd2', 'e2', 'a1', 'b0', 'a2', 'b1', 'a3', 'd3', 'd5', 'b2', 'a4', 'b3', 'a5', 'a6', 'b5']
GATES = {'b0': ('a1',), 'a0': ('d1', 'e1'), 'kb': ('e2',)}
RINGS = {'a': True, 'b': False, 'd': False}
SPLIT = 2
FAR = {'a': True, 'b': False, 'd': False}
JOINT = False


def on_device(layer_input, pre_act, cotangent, down_weight, lengths):
    table = destination_table()
    replica = lax.axis_index("rep").reshape(1)
    got = {}

    def wait(name, value):
        return gate(value, [got[other] for other in GATES.get(name, ())])

    places = [tuple(range(RING // 2)), tuple(range(RING // 2, RING))]
    kept, sent, sums, firsts, ends, blocks = {}, {}, {}, {}, {}, {}
    kept["d"], sent["d"], ordered, masked = down_call(
        table, pre_act, places[0], lengths, layer_input, cotangent
    )
    kept["e"], sent["e"] = down_call(table, pre_act, places[1], masked=masked)
    split = pre_act.shape[1] // 4 * SPLIT

    def core(name):
        if name == "a":
            kept[name], sent[name] = up_call(
                wait("ka", ordered), masked, pre_act, down_weight, 0, split
            )
        if name == "b":
            kept[name], sent[name] = up_call(
                wait("kb", ordered), masked, pre_act, down_weight, split, pre_act.shape[1] - split
            )
        return inner_permute(wait(name + "0", sent[name]), core_route())

    def first(name):
        extra = [sent["e"]] if name == "d" else []
        other = gate(got[name + "0"], [got[o] for o in GATES.get(name + "1", ())] + extra)
        sums[name] = core_sum(kept[name], other)
        return ring_start(sums[name], 0)

    def second(name):
        return ring_pass(sums[name], 0, wait(name + "2", got[name + "1"]))

    def third(name):
        parts = {"d": "de", "a": "ab" if JOINT else "a"}.get(name, name)
        passed = wait(name + "3", [got[part + "2"] for part in parts])
        found = [ring_end(sums[part], got[part + "1"], two) for part, two in zip(parts, passed)]
        if name == "d":
            count = RING // len(parts)
            ends[name] = [
                lambda l, h=h: found[l // count][h](l % count) for h in range(HALVES)
            ]
        elif len(parts) > 1:
            ends[name] = [
                lambda l, h=h: jnp.stack([part[h](l) for part in found]) for h in range(HALVES)
            ]
        else:
            ends[name] = found[0]
        if RINGS[name]:
            return ring_start(once_reduced(ends[name]), 1)
        return direct(ends[name])

    def fourth(name):
        return ring_pass(once_reduced(ends[name]), 1, wait(name + "4", got[name + "3"]))

    def near(name):
        if RINGS[name]:
            last = wait(name + "5", got[name + "4"])
            blocks[name] = joined(ring_end(once_reduced(ends[name]), got[name + "3"], last))
        else:
            blocks[name] = direct_end(ends[name], wait(name + "5", got[name + "3"]))
        if FAR[name]:
            return neighbours(blocks[name])
        return across_replicas(blocks[name])[1:]

    def far(name):
        return opposite(wait(name + "6", got[name + "5"]))

    steps = [core, first, second, third, fourth, near, far]
    for item in ORDER:
        got[item] = steps[int(item[1])](item[0])
    groups = [
        held_blocks(blocks[name], got[name + "5"], got[name + "6"]) if FAR[name]
        else [blocks[name], *got[name + "5"]]
        for name in ("a" if JOINT else "ab") + "d"
    ]
    groups = [[x.reshape(-1, x.shape[-1]) for x in held] for held in groups]
    totals = sum_inner(jnp.stack([products_call(replica, held) for held in groups]))
    rows = layer_input.shape[1] // (CHIPS * CORES), pre_act.shape[1] // (CHIPS * CORES)
    return tuple(mix_call(replica, totals, rows, [groups[:-1], groups[-1:]]))


def solution(mesh):
    in_specs = (
        P(("inner", "rep"), None),
        P(("inner", "rep"), None),
        P(("inner", "rep"), None),
        P(),
        P(("inner", "rep")),
    )
    out_specs = (P("inner", None), P("inner", None))
    return jax.shard_map(
        on_device, mesh=mesh, in_specs=in_specs, out_specs=out_specs, check_vma=False
    )
```

```python
import functools
import math

import jax
import jax.numpy as jnp
from jax import lax
from jax.experimental import pallas as pl
from jax.experimental.pallas import tpu as pltpu
from jax.sharding import PartitionSpec as P

SEQ = 128
RING = 4
CORES = 2
CHIPS = RING * RING
HALVES = 2
LANES = 128
FF_BLOCK = 512
MIB = 1024 * 1024

EPSILON = 1e-06
SQRT_HALF = 0.7071067811865476
INV_ROOT_TWO_PI = 0.3989422804014327
EXP2_SCALE = -0.5 / math.log(2.0)
TERMS = 14
TERM_ROWS = 16


def device_of(y, z, core):
    return (y % RING * RING + z % RING) * CORES + core


def inner_route(move):
    route = []
    for y in range(RING):
        for z in range(RING):
            for core in range(CORES):
                route.append((device_of(y, z, core), device_of(*move(y, z, core))))
    return route


def ring_route(stage, step):
    return inner_route(
        lambda y, z, core: (y + step, z, core) if core == stage else (y, z + step, core)
    )


def core_route():
    return inner_route(lambda y, z, core: (y, z, 1 - core))


def inner_permute(block, route):
    return lax.ppermute(block, "inner", route)


def ring_start(piece, stage):
    return (
        inner_permute(jnp.stack([piece(2, 0), piece(1, 1)]), ring_route(stage, 1)),
        inner_permute(jnp.stack([piece(2, 1), piece(3, 0)]), ring_route(stage, -1)),
    )


def ring_pass(piece, stage, received):
    from_behind, from_ahead = received
    return (
        inner_permute(piece(1, 0) + from_behind[0], ring_route(stage, 1)),
        inner_permute(piece(3, 1) + from_ahead[0], ring_route(stage, -1)),
    )


def ring_end(piece, received, passed):
    from_behind, from_ahead = received
    return (
        lambda at: piece(0, 0)[at] + from_ahead[1][at] + passed[0][at],
        lambda at: piece(0, 1)[at] + from_behind[1][at] + passed[1][at],
    )


def once_reduced(halves):
    return lambda l, h: halves[h](l)


def joined(halves):
    return jnp.concatenate([half(...) for half in halves], axis=-2)


def direct(halves):
    return [
        inner_permute(jnp.stack([half(step) for half in halves]), ring_route(1, step))
        for step in range(1, RING)
    ]


def direct_end(halves, received):
    one, two, three = received
    return jnp.concatenate(
        [(half(0) + two[h]) + (one[h] + three[h]) for h, half in enumerate(halves)], axis=-2
    )


def core_sum(keep, other):
    return lambda k, h: keep[k, h] + other[k, h]


def gate(arrived, earlier=()):
    return lax.optimization_barrier((arrived, earlier))[0]


def destination_table():
    inner = lax.axis_index("inner")
    y, z, core = inner // (RING * CORES), inner // CORES % RING, inner % CORES
    k = lax.iota(jnp.int32, RING)[:, None]
    l = lax.iota(jnp.int32, RING)[None, :]

    def order(core_to):
        to_y = jnp.where(core_to == 0, y + k, y + l) % RING
        to_z = jnp.where(core_to == 0, z + l, z + k) % RING
        return (to_y * RING + to_z) * CORES + core_to

    return jnp.stack([order(core), order(1 - core)])


def write_masked(lengths_ref, cotangent_ref, masked_ref):
    columns = cotangent_ref.shape[1]
    for seq in range(cotangent_ref.shape[0] // SEQ):
        rows = slice(seq * SEQ, (seq + 1) * SEQ)
        valid = lax.broadcasted_iota(jnp.int32, (SEQ, columns), 0) < lengths_ref[seq]
        values = cotangent_ref[rows, :].astype(jnp.float32)
        masked_ref[rows, :] = jnp.where(valid, values, 0.0).astype(masked_ref.dtype)


def down_blocks(pre_refs, masked_ref, keep_ref, send_ref):
    rows = pre_refs[0].shape[1]
    for first in range(0, len(pre_refs), 2):
        columns = []
        for ref in pre_refs[first:first + 2]:
            value = ref[...].astype(jnp.float32)
            cdf = 0.5 + 0.5 * lax.erf(value * SQRT_HALF)
            columns.append((value * cdf).astype(jnp.bfloat16))
        product = lax.dot_general(
            jnp.concatenate(columns, axis=1), masked_ref[...], (((0,), (0,)), ((), ())),
            preferred_element_type=jnp.float32,
        )
        for index in range(2):
            which, place = divmod(first + index, len(pre_refs) // 2)
            out_ref = (keep_ref, send_ref)[which]
            part = product[index * rows:(index + 1) * rows]
            out_ref[0, :, place, :, :] = part.reshape(HALVES, rows // HALVES, part.shape[1])


def first_down_kernel(blocks_ref, lengths_ref, cotangent_ref, *refs):
    pre_refs, (keep_ref, send_ref, masked_ref) = refs[:-3], refs[-3:]

    @pl.when(pl.program_id(0) == 0)
    def _():
        write_masked(lengths_ref, cotangent_ref, masked_ref)

    down_blocks(pre_refs, masked_ref, keep_ref, send_ref)


def down_kernel(blocks_ref, masked_ref, *refs):
    down_blocks(refs[:-2], masked_ref, *refs[-2:])


def down_call(table, pre_act, places, lengths=None, cotangent=None, masked=None):
    is_first = masked is None
    tokens, width = (cotangent if is_first else masked).shape
    rows = pre_act.shape[1] // (CHIPS * CORES)

    def pre_spec(which, place):
        return pl.BlockSpec(
            (tokens, rows), lambda k, blocks_ref, *_: (0, blocks_ref[which * CHIPS + k * RING + place])
        )

    whole = pl.BlockSpec((tokens, width), lambda k, *_: (0, 0))
    out_block = pl.BlockSpec(
        (1, HALVES, len(places), rows // HALVES, width), lambda k, *_: (k, 0, 0, 0, 0)
    )
    out_shape = [
        jax.ShapeDtypeStruct((RING, HALVES, len(places), rows // HALVES, width), jnp.float32)
    ] * 2
    prefetch, wholes, extra = [table.reshape(-1)], [masked], []
    if is_first:
        prefetch, wholes, extra = prefetch + [lengths], [cotangent], [whole]
        out_shape = out_shape + [jax.ShapeDtypeStruct((tokens, width), jnp.bfloat16)]
    count = 2 * len(places)
    return pl.pallas_call(
        first_down_kernel if is_first else down_kernel,
        grid_spec=pltpu.PrefetchScalarGridSpec(
            num_scalar_prefetch=len(prefetch),
            grid=(RING,),
            in_specs=[whole] * len(wholes)
            + [pre_spec(which, place) for which in range(2) for place in places],
            out_specs=[out_block, out_block] + extra,
        ),
        out_shape=out_shape,
        compiler_params=pltpu.CompilerParams(vmem_limit_bytes=60 * MIB),
        cost_estimate=pl.CostEstimate(
            flops=2 * tokens * width * rows * RING * count,
            bytes_accessed=4 * tokens * width + (2 * tokens + 4 * width) * rows * RING * count,
            transcendentals=0,
        ),
        name="down_partial",
    )(*prefetch, *wholes, *[pre_act] * count)


def up_columns(ordered_ref, masked_ref, pre_ref, weight_ref, keep_ref, send_ref):
    tokens, width = masked_ref.shape
    grads = []
    part = tokens // 4
    for first in range(0, tokens, part):
        rows = slice(first, first + part)
        hidden_grad = lax.dot_general(
            masked_ref[rows, :], weight_ref[...], (((1,), (1,)), ((), ())),
            preferred_element_type=jnp.float32,
        )
        value = pre_ref[rows, :].astype(jnp.float32)
        cdf = 0.5 + 0.5 * lax.erf(value * SQRT_HALF)
        density = jnp.exp2(value * value * EXP2_SCALE)
        derivative = cdf + value * density * INV_ROOT_TWO_PI
        grads.append((hidden_grad * derivative).astype(jnp.bfloat16))
    grad = jnp.concatenate(grads, axis=0)
    half = width // CORES
    keep_ref[...] = jnp.dot(ordered_ref[:half, :], grad, preferred_element_type=jnp.float32)
    send_ref[...] = jnp.dot(ordered_ref[half:, :], grad, preferred_element_type=jnp.float32)


def first_up_kernel(rows_ref, x_ref, masked_ref, pre_ref, weight_ref,
                    keep_ref, send_ref, ordered_ref, turned_ref):
    @pl.when(pl.program_id(0) == 0)
    def _():
        strip = x_ref.shape[1] // (CHIPS * CORES * HALVES)
        turned_ref[...] = x_ref[...].T
        for index in range(x_ref.shape[1] // strip):
            start = pl.multiple_of(rows_ref[index], strip)
            ordered_ref[index * strip:(index + 1) * strip, :] = turned_ref[pl.ds(start, strip), :]

    up_columns(ordered_ref, masked_ref, pre_ref, weight_ref, keep_ref, send_ref)


def up_kernel(rows_ref, ordered_ref, masked_ref, pre_ref, weight_ref, keep_ref, send_ref):
    up_columns(ordered_ref, masked_ref, pre_ref, weight_ref, keep_ref, send_ref)


def up_call(table, x, ordered, masked, pre_act, weight, start, count):
    is_first = ordered is None
    tokens, width = masked.shape
    strip = width // (CHIPS * CORES * HALVES)
    half = lax.iota(jnp.int32, HALVES)[None, None, :, None]
    strips = (table[:, :, None, :] * HALVES + half).reshape(-1) * strip
    at = start // FF_BLOCK
    turned = pl.BlockSpec((width, tokens), lambda j, *_: (0, 0))
    whole = pl.BlockSpec((tokens, width), lambda j, *_: (0, 0))
    out_block = pl.BlockSpec((width // CORES, FF_BLOCK), lambda j, *_: (0, j))
    out_shape = [jax.ShapeDtypeStruct((width // CORES, count), jnp.float32)] * 2
    if is_first:
        out_shape = out_shape + [jax.ShapeDtypeStruct((width, tokens), jnp.bfloat16)]
    keep, send, *ordered_out = pl.pallas_call(
        first_up_kernel if is_first else up_kernel,
        grid_spec=pltpu.PrefetchScalarGridSpec(
            num_scalar_prefetch=1,
            grid=(count // FF_BLOCK,),
            in_specs=[
                whole if is_first else turned,
                whole,
                pl.BlockSpec((tokens, FF_BLOCK), lambda j, *_: (0, at + j)),
                pl.BlockSpec((FF_BLOCK, width), lambda j, *_: (at + j, 0)),
            ],
            out_specs=[out_block, out_block] + [turned] * is_first,
            scratch_shapes=[pltpu.VMEM((width, tokens), jnp.bfloat16)] * is_first,
        ),
        out_shape=out_shape,
        compiler_params=pltpu.CompilerParams(vmem_limit_bytes=40 * MIB),
        cost_estimate=pl.CostEstimate(
            flops=4 * tokens * width * count,
            bytes_accessed=4 * tokens * width + 2 * tokens * count + 6 * width * count,
            transcendentals=2 * tokens * count,
        ),
        name="up_partial",
    )(strips, x if is_first else ordered, masked, pre_act, weight)
    shape = (RING, HALVES, RING, strip, count)
    return keep.reshape(shape), send.reshape(shape), *ordered_out


def replica_route(step):
    count = lax.axis_size("rep")
    return [(i, (i + step) % count) for i in range(count)]


def neighbours(block):
    return tuple(lax.ppermute(block, "rep", replica_route(step)) for step in (1, -1))


def opposite(received):
    from_behind, from_ahead = received
    half = from_behind.shape[0] // 2
    return (
        lax.ppermute(from_behind[:half], "rep", replica_route(1)),
        lax.ppermute(from_ahead[half:], "rep", replica_route(-1)),
    )


def held_blocks(block, received, far):
    return [block, received[1], jnp.concatenate(far, axis=0), received[0]]


def across_replicas(block):
    return [block] + [lax.ppermute(block, "rep", replica_route(-step)) for step in range(1, RING)]


def in_order(values, replica):
    once = [jnp.where(replica % 2 == 1, values[i - 1], values[i]) for i in range(4)]
    return [jnp.where(replica // 2 == 1, once[i - 2], once[i]) for i in range(4)]


def products_kernel(replica_ref, *refs):
    held, out_ref = refs[:-1], refs[-1]
    replica = replica_ref[0]
    rows, columns = held[0].shape[-2:]

    def add_rows(index, totals):
        at = pl.ds(pl.multiple_of(index * 8, 8), 8)
        sums = [totals[i * 8:(i + 1) * 8, :] for i in range(TERMS)]
        for column in range(0, columns, LANES):
            a, d, b, e = in_order(
                [ref[at, column:column + LANES] for ref in held], replica
            )
            terms = []
            for left, right in ((a, b), (d, e)):
                both = left + right
                terms += [left * left, right * right, left * right, both * both,
                          both * (left - right)]
            terms += [a * d, a * e, b * d, b * e]
            sums = [total + term for total, term in zip(sums, terms)]
        return jnp.concatenate(sums, axis=0)

    totals = lax.fori_loop(0, rows // 8, add_rows, jnp.zeros((TERMS * 8, LANES), jnp.float32))
    for i in range(TERMS):
        out_ref[i:i + 1, :] = jnp.sum(totals[i * 8:(i + 1) * 8, :], axis=0, keepdims=True)
    out_ref[TERMS:, :] = jnp.zeros((TERM_ROWS - TERMS, LANES), jnp.float32)


def products_call(replica, held):
    vmem = pl.BlockSpec(memory_space=pltpu.VMEM)
    return pl.pallas_call(
        products_kernel,
        in_specs=[pl.BlockSpec(memory_space=pltpu.SMEM)] + [vmem] * len(held),
        out_specs=vmem,
        out_shape=jax.ShapeDtypeStruct((TERM_ROWS, LANES), jnp.float32),
        compiler_params=pltpu.CompilerParams(vmem_limit_bytes=24 * MIB),
        cost_estimate=pl.CostEstimate(
            flops=TERMS * 2 * held[0].size, bytes_accessed=16 * held[0].size, transcendentals=0
        ),
        name="inner_products",
    )(replica, *held)


def sum_inner(values):
    values = values + inner_permute(values, core_route())
    for axis in (0, 1):
        others = [
            inner_permute(values, inner_route(
                lambda y, z, core: (y + step, z, core) if axis == 0 else (y, z + step, core)))
            for step in (1, 2, 3)
        ]
        values = (values + others[1]) + (others[0] + others[2])
    return values


def pair_coefs(first_sq, second_sq, cross, both_sq, difference):
    first_wide, second_wide = first_sq + EPSILON, second_sq + EPSILON
    first_coef = 1.0 - cross / (2.0 * first_wide)
    second_coef = 1.0 - cross / (2.0 * second_wide)
    plain = (first_coef * first_coef * first_sq + 2.0 * first_coef * second_coef * cross
             + second_coef * second_coef * second_sq)
    mean = 0.5 * (first_coef + second_coef)
    skew = 0.25 * (cross / first_wide) * (difference / second_wide)
    apart = first_sq + second_sq - 2.0 * cross
    opposite = mean * mean * both_sq + 2.0 * mean * skew * difference + skew * skew * apart
    square = jnp.where(both_sq < 0.25 * (first_sq + second_sq), opposite, plain)
    return first_coef, second_coef, square


def coefficients(t):
    a, b, left = pair_coefs(*t[0:5])
    d, e, right = pair_coefs(*t[5:10])
    cross = a * (d * t[10] + e * t[11]) + b * (d * t[12] + e * t[13])
    left_coef = 1.0 - cross / (2.0 * (left + EPSILON))
    right_coef = 1.0 - cross / (2.0 * (right + EPSILON))
    return left_coef * a, right_coef * d, left_coef * b, right_coef * e


def mix_kernel(counts, replica_ref, totals_ref, *refs):
    groups, outs = refs[:-len(counts)], refs[-len(counts):]
    replica = replica_ref[0]
    group = 0
    for count, out_ref in zip(counts, outs):
        totals = totals_ref[group]
        for index in range(1, count):
            totals = totals + totals_ref[group + index]
        totals = jnp.sum(totals, axis=1, keepdims=True)
        coefs = coefficients([totals[i:i + 1, :] for i in range(TERMS)])
        start = 0
        for index in range(group, group + count):
            held = groups[4 * index:4 * index + 4]
            rows, columns = out_ref.shape[0], held[0].shape[1]
            for first in range(0, held[0].shape[0], rows):
                values = in_order([ref[first:first + rows, :] for ref in held], replica)
                a, d, b, e = [value * coef for value, coef in zip(values, coefs)]
                out_ref[:, start:start + columns] = (a + b) + (d + e)
                start += columns
        group += count


def mix_call(replica, totals, rows, outs):
    vmem = pl.BlockSpec(memory_space=pltpu.VMEM)
    flat = [block for groups in outs for held in groups for block in held]
    shapes = [
        jax.ShapeDtypeStruct((count, sum(held[0].size for held in groups) // count), jnp.float32)
        for count, groups in zip(rows, outs)
    ]
    size = sum(shape.size for shape in shapes)
    return pl.pallas_call(
        functools.partial(mix_kernel, [len(groups) for groups in outs]),
        in_specs=[pl.BlockSpec(memory_space=pltpu.SMEM)] + [vmem] * (len(flat) + 1),
        out_specs=[vmem] * len(shapes),
        out_shape=shapes,
        compiler_params=pltpu.CompilerParams(vmem_limit_bytes=24 * MIB),
        cost_estimate=pl.CostEstimate(flops=7 * size, bytes_accessed=20 * size, transcendentals=0),
        name="combine",
    )(replica, totals, *flat)


ORDER = ['d0', 'd1', 'e0', 'e1', 'a0', 'd2', 'e2', 'a1', 'b0', 'a2', 'b1', 'a3', 'd3', 'd5', 'b2', 'a4', 'b3', 'a5', 'a6', 'b5']
GATES = {'b0': ('a1',), 'a0': ('d1', 'e1'), 'kb': ('e2',)}
RINGS = {'a': True, 'b': False, 'd': False}
SPLIT = 4
FAR = {'a': True, 'b': False, 'd': False}
JOINT = False


def on_device(layer_input, pre_act, cotangent, down_weight, lengths):
    table = destination_table()
    replica = lax.axis_index("rep").reshape(1)
    got = {}

    def wait(name, value):
        return gate(value, [got[other] for other in GATES.get(name, ())])

    places = [tuple(range(RING // 2)), tuple(range(RING // 2, RING))]
    kept, sent, sums, firsts, ends, blocks = {}, {}, {}, {}, {}, {}
    kept["d"], sent["d"], masked = down_call(table, pre_act, places[0], lengths, cotangent)
    kept["e"], sent["e"] = down_call(table, pre_act, places[1], masked=masked)
    split = pre_act.shape[1] // 8 * SPLIT

    def core(name):
        if name == "a":
            kept[name], sent[name], sent["x"] = up_call(
                table, layer_input, None, wait("ka", masked), pre_act, down_weight, 0, split
            )
        if name == "b":
            kept[name], sent[name] = up_call(
                table, layer_input, wait("kb", sent["x"]), masked, pre_act, down_weight,
                split, pre_act.shape[1] - split,
            )
        return inner_permute(wait(name + "0", sent[name]), core_route())

    def first(name):
        extra = [sent["e"]] if name == "d" else []
        other = gate(got[name + "0"], [got[o] for o in GATES.get(name + "1", ())] + extra)
        sums[name] = core_sum(kept[name], other)
        return ring_start(sums[name], 0)

    def second(name):
        return ring_pass(sums[name], 0, wait(name + "2", got[name + "1"]))

    def third(name):
        parts = {"d": "de", "a": "ab" if JOINT else "a"}.get(name, name)
        passed = wait(name + "3", [got[part + "2"] for part in parts])
        found = [ring_end(sums[part], got[part + "1"], two) for part, two in zip(parts, passed)]
        if name == "d":
            count = RING // len(parts)
            ends[name] = [
                lambda l, h=h: found[l // count][h](l % count) for h in range(HALVES)
            ]
        elif len(parts) > 1:
            ends[name] = [
                lambda l, h=h: jnp.stack([part[h](l) for part in found]) for h in range(HALVES)
            ]
        else:
            ends[name] = found[0]
        if RINGS[name]:
            return ring_start(once_reduced(ends[name]), 1)
        return direct(ends[name])

    def fourth(name):
        return ring_pass(once_reduced(ends[name]), 1, wait(name + "4", got[name + "3"]))

    def near(name):
        if RINGS[name]:
            last = wait(name + "5", got[name + "4"])
            blocks[name] = joined(ring_end(once_reduced(ends[name]), got[name + "3"], last))
        else:
            blocks[name] = direct_end(ends[name], wait(name + "5", got[name + "3"]))
        if FAR[name]:
            return neighbours(blocks[name])
        return across_replicas(blocks[name])[1:]

    def far(name):
        return opposite(wait(name + "6", got[name + "5"]))

    steps = [core, first, second, third, fourth, near, far]
    for item in ORDER:
        got[item] = steps[int(item[1])](item[0])
    groups = [
        held_blocks(blocks[name], got[name + "5"], got[name + "6"]) if FAR[name]
        else [blocks[name], *got[name + "5"]]
        for name in ("a" if JOINT else "ab") + "d"
    ]
    groups = [[x.reshape(-1, x.shape[-1]) for x in held] for held in groups]
    totals = sum_inner(jnp.stack([products_call(replica, held) for held in groups]))
    rows = layer_input.shape[1] // (CHIPS * CORES), pre_act.shape[1] // (CHIPS * CORES)
    return tuple(mix_call(replica, totals, rows, [groups[:-1], groups[-1:]]))


def solution(mesh):
    in_specs = (
        P(("inner", "rep"), None),
        P(("inner", "rep"), None),
        P(("inner", "rep"), None),
        P(),
        P(("inner", "rep")),
    )
    out_specs = (P("inner", None), P("inner", None))
    return jax.shard_map(
        on_device, mesh=mesh, in_specs=in_specs, out_specs=out_specs, check_vma=False
    )
```

```python
import functools
import math

import jax
import jax.numpy as jnp
from jax import lax
from jax.experimental import pallas as pl
from jax.experimental.pallas import tpu as pltpu
from jax.sharding import PartitionSpec as P

SEQ = 128
RING = 4
CORES = 2
CHIPS = RING * RING
HALVES = 2
LANES = 128
FF_BLOCK = 512
MIB = 1024 * 1024

EPSILON = 1e-06
SQRT_HALF = 0.7071067811865476
INV_ROOT_TWO_PI = 0.3989422804014327
EXP2_SCALE = -0.5 / math.log(2.0)
TERMS = 14
TERM_ROWS = 16


def device_of(y, z, core):
    return (y % RING * RING + z % RING) * CORES + core


def inner_route(move):
    route = []
    for y in range(RING):
        for z in range(RING):
            for core in range(CORES):
                route.append((device_of(y, z, core), device_of(*move(y, z, core))))
    return route


def ring_route(stage, step):
    return inner_route(
        lambda y, z, core: (y + step, z, core) if core == stage else (y, z + step, core)
    )


def core_route():
    return inner_route(lambda y, z, core: (y, z, 1 - core))


def inner_permute(block, route):
    return lax.ppermute(block, "inner", route)


def ring_start(piece, stage):
    return (
        inner_permute(jnp.stack([piece(2, 0), piece(1, 1)]), ring_route(stage, 1)),
        inner_permute(jnp.stack([piece(2, 1), piece(3, 0)]), ring_route(stage, -1)),
    )


def ring_pass(piece, stage, received):
    from_behind, from_ahead = received
    return (
        inner_permute(piece(1, 0) + from_behind[0], ring_route(stage, 1)),
        inner_permute(piece(3, 1) + from_ahead[0], ring_route(stage, -1)),
    )


def ring_end(piece, received, passed):
    from_behind, from_ahead = received
    return (
        lambda at: piece(0, 0)[at] + from_ahead[1][at] + passed[0][at],
        lambda at: piece(0, 1)[at] + from_behind[1][at] + passed[1][at],
    )


def once_reduced(halves):
    return lambda l, h: halves[h](l)


def joined(halves):
    return jnp.concatenate([half(...) for half in halves], axis=-2)


def direct(halves):
    return [
        inner_permute(jnp.stack([half(step) for half in halves]), ring_route(1, step))
        for step in range(1, RING)
    ]


def direct_end(halves, received):
    one, two, three = received
    return jnp.concatenate(
        [(half(0) + two[h]) + (one[h] + three[h]) for h, half in enumerate(halves)], axis=-2
    )


def core_sum(keep, other):
    return lambda k, h: keep[k, h] + other[k, h]


def gate(arrived, earlier=()):
    return lax.optimization_barrier((arrived, earlier))[0]


def destination_table():
    inner = lax.axis_index("inner")
    y, z, core = inner // (RING * CORES), inner // CORES % RING, inner % CORES
    k = lax.iota(jnp.int32, RING)[:, None]
    l = lax.iota(jnp.int32, RING)[None, :]

    def order(core_to):
        to_y = jnp.where(core_to == 0, y + k, y + l) % RING
        to_z = jnp.where(core_to == 0, z + l, z + k) % RING
        return (to_y * RING + to_z) * CORES + core_to

    return jnp.stack([order(core), order(1 - core)])


def write_masked(lengths_ref, cotangent_ref, masked_ref):
    columns = cotangent_ref.shape[1]
    for seq in range(cotangent_ref.shape[0] // SEQ):
        rows = slice(seq * SEQ, (seq + 1) * SEQ)
        valid = lax.broadcasted_iota(jnp.int32, (SEQ, columns), 0) < lengths_ref[seq]
        values = cotangent_ref[rows, :].astype(jnp.float32)
        masked_ref[rows, :] = jnp.where(valid, values, 0.0).astype(masked_ref.dtype)


def down_blocks(pre_refs, masked_ref, keep_ref, send_ref):
    rows = pre_refs[0].shape[1]
    for first in range(0, len(pre_refs), 2):
        columns = []
        for ref in pre_refs[first:first + 2]:
            value = ref[...].astype(jnp.float32)
            cdf = 0.5 + 0.5 * lax.erf(value * SQRT_HALF)
            columns.append((value * cdf).astype(jnp.bfloat16))
        product = lax.dot_general(
            jnp.concatenate(columns, axis=1), masked_ref[...], (((0,), (0,)), ((), ())),
            preferred_element_type=jnp.float32,
        )
        for index in range(2):
            which, place = divmod(first + index, len(pre_refs) // 2)
            out_ref = (keep_ref, send_ref)[which]
            part = product[index * rows:(index + 1) * rows]
            out_ref[0, :, place, :, :] = part.reshape(HALVES, rows // HALVES, part.shape[1])


def first_down_kernel(blocks_ref, lengths_ref, cotangent_ref, *refs):
    pre_refs, (keep_ref, send_ref, masked_ref) = refs[:-3], refs[-3:]

    @pl.when(pl.program_id(0) == 0)
    def _():
        write_masked(lengths_ref, cotangent_ref, masked_ref)

    down_blocks(pre_refs, masked_ref, keep_ref, send_ref)


def down_kernel(blocks_ref, masked_ref, *refs):
    down_blocks(refs[:-2], masked_ref, *refs[-2:])


def down_call(table, pre_act, places, lengths=None, cotangent=None, masked=None):
    is_first = masked is None
    tokens, width = (cotangent if is_first else masked).shape
    rows = pre_act.shape[1] // (CHIPS * CORES)

    def pre_spec(which, place):
        return pl.BlockSpec(
            (tokens, rows), lambda k, blocks_ref, *_: (0, blocks_ref[which * CHIPS + k * RING + place])
        )

    whole = pl.BlockSpec((tokens, width), lambda k, *_: (0, 0))
    out_block = pl.BlockSpec(
        (1, HALVES, len(places), rows // HALVES, width), lambda k, *_: (k, 0, 0, 0, 0)
    )
    out_shape = [
        jax.ShapeDtypeStruct((RING, HALVES, len(places), rows // HALVES, width), jnp.float32)
    ] * 2
    prefetch, wholes, extra = [table.reshape(-1)], [masked], []
    if is_first:
        prefetch, wholes, extra = prefetch + [lengths], [cotangent], [whole]
        out_shape = out_shape + [jax.ShapeDtypeStruct((tokens, width), jnp.bfloat16)]
    count = 2 * len(places)
    return pl.pallas_call(
        first_down_kernel if is_first else down_kernel,
        grid_spec=pltpu.PrefetchScalarGridSpec(
            num_scalar_prefetch=len(prefetch),
            grid=(RING,),
            in_specs=[whole] * len(wholes)
            + [pre_spec(which, place) for which in range(2) for place in places],
            out_specs=[out_block, out_block] + extra,
        ),
        out_shape=out_shape,
        compiler_params=pltpu.CompilerParams(vmem_limit_bytes=24 * MIB),
        cost_estimate=pl.CostEstimate(
            flops=2 * tokens * width * rows * RING * count,
            bytes_accessed=4 * tokens * width + (2 * tokens + 4 * width) * rows * RING * count,
            transcendentals=0,
        ),
        name="down_partial",
    )(*prefetch, *wholes, *[pre_act] * count)


def up_columns(ordered_ref, masked_ref, pre_ref, weight_ref, keep_ref, send_ref):
    tokens, width = masked_ref.shape
    grads = []
    part = tokens // 4
    for first in range(0, tokens, part):
        rows = slice(first, first + part)
        hidden_grad = lax.dot_general(
            masked_ref[rows, :], weight_ref[...], (((1,), (1,)), ((), ())),
            preferred_element_type=jnp.float32,
        )
        value = pre_ref[rows, :].astype(jnp.float32)
        cdf = 0.5 + 0.5 * lax.erf(value * SQRT_HALF)
        density = jnp.exp2(value * value * EXP2_SCALE)
        derivative = cdf + value * density * INV_ROOT_TWO_PI
        grads.append((hidden_grad * derivative).astype(jnp.bfloat16))
    grad = jnp.concatenate(grads, axis=0)
    half = width // CORES
    keep_ref[...] = jnp.dot(ordered_ref[:half, :], grad, preferred_element_type=jnp.float32)
    send_ref[...] = jnp.dot(ordered_ref[half:, :], grad, preferred_element_type=jnp.float32)


def first_up_kernel(rows_ref, x_ref, masked_ref, pre_ref, weight_ref,
                    keep_ref, send_ref, ordered_ref, turned_ref):
    @pl.when(pl.program_id(0) == 0)
    def _():
        strip = x_ref.shape[1] // (CHIPS * CORES * HALVES)
        turned_ref[...] = x_ref[...].T
        for index in range(x_ref.shape[1] // strip):
            start = pl.multiple_of(rows_ref[index], strip)
            ordered_ref[index * strip:(index + 1) * strip, :] = turned_ref[pl.ds(start, strip), :]

    up_columns(ordered_ref, masked_ref, pre_ref, weight_ref, keep_ref, send_ref)


def up_kernel(rows_ref, ordered_ref, masked_ref, pre_ref, weight_ref, keep_ref, send_ref):
    up_columns(ordered_ref, masked_ref, pre_ref, weight_ref, keep_ref, send_ref)


def up_call(table, x, ordered, masked, pre_act, weight, start, count):
    is_first = ordered is None
    tokens, width = masked.shape
    strip = width // (CHIPS * CORES * HALVES)
    half = lax.iota(jnp.int32, HALVES)[None, None, :, None]
    strips = (table[:, :, None, :] * HALVES + half).reshape(-1) * strip
    at = start // FF_BLOCK
    turned = pl.BlockSpec((width, tokens), lambda j, *_: (0, 0))
    whole = pl.BlockSpec((tokens, width), lambda j, *_: (0, 0))
    out_block = pl.BlockSpec((width // CORES, FF_BLOCK), lambda j, *_: (0, j))
    out_shape = [jax.ShapeDtypeStruct((width // CORES, count), jnp.float32)] * 2
    if is_first:
        out_shape = out_shape + [jax.ShapeDtypeStruct((width, tokens), jnp.bfloat16)]
    keep, send, *ordered_out = pl.pallas_call(
        first_up_kernel if is_first else up_kernel,
        grid_spec=pltpu.PrefetchScalarGridSpec(
            num_scalar_prefetch=1,
            grid=(count // FF_BLOCK,),
            in_specs=[
                whole if is_first else turned,
                whole,
                pl.BlockSpec((tokens, FF_BLOCK), lambda j, *_: (0, at + j)),
                pl.BlockSpec((FF_BLOCK, width), lambda j, *_: (at + j, 0)),
            ],
            out_specs=[out_block, out_block] + [turned] * is_first,
            scratch_shapes=[pltpu.VMEM((width, tokens), jnp.bfloat16)] * is_first,
        ),
        out_shape=out_shape,
        compiler_params=pltpu.CompilerParams(vmem_limit_bytes=34 * MIB),
        cost_estimate=pl.CostEstimate(
            flops=12 * tokens * width * count,
            bytes_accessed=4 * tokens * width + 2 * tokens * count + 6 * width * count,
            transcendentals=2 * tokens * count,
        ),
        name="up_partial",
    )(strips, x if is_first else ordered, masked, pre_act, weight)
    shape = (RING, HALVES, RING, strip, count)
    return keep.reshape(shape), send.reshape(shape), *ordered_out


def replica_route(step):
    count = lax.axis_size("rep")
    return [(i, (i + step) % count) for i in range(count)]


def neighbours(block):
    return tuple(lax.ppermute(block, "rep", replica_route(step)) for step in (1, -1))


def opposite(received):
    from_behind, from_ahead = received
    half = from_behind.shape[0] // 2
    return (
        lax.ppermute(from_behind[:half], "rep", replica_route(1)),
        lax.ppermute(from_ahead[half:], "rep", replica_route(-1)),
    )


def held_blocks(block, received, far):
    return [block, received[1], jnp.concatenate(far, axis=0), received[0]]


def across_replicas(block):
    return [block] + [lax.ppermute(block, "rep", replica_route(-step)) for step in range(1, RING)]


def in_order(values, replica):
    once = [jnp.where(replica % 2 == 1, values[i - 1], values[i]) for i in range(4)]
    return [jnp.where(replica // 2 == 1, once[i - 2], once[i]) for i in range(4)]


def products_kernel(replica_ref, *refs):
    held, out_ref = refs[:-1], refs[-1]
    replica = replica_ref[0]
    rows, columns = held[0].shape[-2:]

    def add_rows(index, totals):
        at = pl.ds(pl.multiple_of(index * 8, 8), 8)
        sums = [totals[i * 8:(i + 1) * 8, :] for i in range(TERMS)]
        for column in range(0, columns, LANES):
            a, d, b, e = in_order(
                [ref[at, column:column + LANES] for ref in held], replica
            )
            terms = []
            for left, right in ((a, b), (d, e)):
                both = left + right
                terms += [left * left, right * right, left * right, both * both,
                          both * (left - right)]
            terms += [a * d, a * e, b * d, b * e]
            sums = [total + term for total, term in zip(sums, terms)]
        return jnp.concatenate(sums, axis=0)

    totals = lax.fori_loop(0, rows // 8, add_rows, jnp.zeros((TERMS * 8, LANES), jnp.float32))
    for i in range(TERMS):
        out_ref[i:i + 1, :] = jnp.sum(totals[i * 8:(i + 1) * 8, :], axis=0, keepdims=True)
    out_ref[TERMS:, :] = jnp.zeros((TERM_ROWS - TERMS, LANES), jnp.float32)


def products_call(replica, held):
    vmem = pl.BlockSpec(memory_space=pltpu.VMEM)
    return pl.pallas_call(
        products_kernel,
        in_specs=[pl.BlockSpec(memory_space=pltpu.SMEM)] + [vmem] * len(held),
        out_specs=vmem,
        out_shape=jax.ShapeDtypeStruct((TERM_ROWS, LANES), jnp.float32),
        compiler_params=pltpu.CompilerParams(vmem_limit_bytes=24 * MIB),
        cost_estimate=pl.CostEstimate(
            flops=TERMS * 2 * held[0].size, bytes_accessed=16 * held[0].size, transcendentals=0
        ),
        name="inner_products",
    )(replica, *held)


def sum_inner(values):
    values = values + inner_permute(values, core_route())
    for axis in (0, 1):
        others = [
            inner_permute(values, inner_route(
                lambda y, z, core: (y + step, z, core) if axis == 0 else (y, z + step, core)))
            for step in (1, 2, 3)
        ]
        values = (values + others[1]) + (others[0] + others[2])
    return values


def pair_coefs(first_sq, second_sq, cross, both_sq, difference):
    first_wide, second_wide = first_sq + EPSILON, second_sq + EPSILON
    first_coef = 1.0 - cross / (2.0 * first_wide)
    second_coef = 1.0 - cross / (2.0 * second_wide)
    plain = (first_coef * first_coef * first_sq + 2.0 * first_coef * second_coef * cross
             + second_coef * second_coef * second_sq)
    mean = 0.5 * (first_coef + second_coef)
    skew = 0.25 * (cross / first_wide) * (difference / second_wide)
    apart = first_sq + second_sq - 2.0 * cross
    opposite = mean * mean * both_sq + 2.0 * mean * skew * difference + skew * skew * apart
    square = jnp.where(both_sq < 0.25 * (first_sq + second_sq), opposite, plain)
    return first_coef, second_coef, square


def coefficients(t):
    a, b, left = pair_coefs(*t[0:5])
    d, e, right = pair_coefs(*t[5:10])
    cross = a * (d * t[10] + e * t[11]) + b * (d * t[12] + e * t[13])
    left_coef = 1.0 - cross / (2.0 * (left + EPSILON))
    right_coef = 1.0 - cross / (2.0 * (right + EPSILON))
    return left_coef * a, right_coef * d, left_coef * b, right_coef * e


def mix_kernel(counts, replica_ref, totals_ref, *refs):
    groups, outs = refs[:-len(counts)], refs[-len(counts):]
    replica = replica_ref[0]
    group = 0
    for count, out_ref in zip(counts, outs):
        totals = totals_ref[group]
        for index in range(1, count):
            totals = totals + totals_ref[group + index]
        totals = jnp.sum(totals, axis=1, keepdims=True)
        coefs = coefficients([totals[i:i + 1, :] for i in range(TERMS)])
        start = 0
        for index in range(group, group + count):
            held = groups[4 * index:4 * index + 4]
            rows, columns = out_ref.shape[0], held[0].shape[1]
            for first in range(0, held[0].shape[0], rows):
                values = in_order([ref[first:first + rows, :] for ref in held], replica)
                a, d, b, e = [value * coef for value, coef in zip(values, coefs)]
                out_ref[:, start:start + columns] = (a + b) + (d + e)
                start += columns
        group += count


def mix_call(replica, totals, rows, outs):
    vmem = pl.BlockSpec(memory_space=pltpu.VMEM)
    flat = [block for groups in outs for held in groups for block in held]
    shapes = [
        jax.ShapeDtypeStruct((count, sum(held[0].size for held in groups) // count), jnp.float32)
        for count, groups in zip(rows, outs)
    ]
    size = sum(shape.size for shape in shapes)
    return pl.pallas_call(
        functools.partial(mix_kernel, [len(groups) for groups in outs]),
        in_specs=[pl.BlockSpec(memory_space=pltpu.SMEM)] + [vmem] * (len(flat) + 1),
        out_specs=[vmem] * len(shapes),
        out_shape=shapes,
        compiler_params=pltpu.CompilerParams(vmem_limit_bytes=24 * MIB),
        cost_estimate=pl.CostEstimate(flops=7 * size, bytes_accessed=20 * size, transcendentals=0),
        name="combine",
    )(replica, totals, *flat)


ORDER = ['d0', 'd1', 'e0', 'e1', 'a0', 'd2', 'e2', 'a1', 'b0', 'a2', 'b1', 'a3', 'd3', 'd5', 'b2', 'a4', 'b3', 'a5', 'a6', 'b5']
GATES = {'a0': ('d1', 'e1'), 'kb': ('a0',), 'b5': ('a5', 'a3'), 'd2': ('e1',)}
RINGS = {'a': True, 'b': False, 'd': False}
SPLIT = 4
FAR = {'a': True, 'b': False, 'd': False}
JOINT = False


def on_device(layer_input, pre_act, cotangent, down_weight, lengths):
    table = destination_table()
    replica = lax.axis_index("rep").reshape(1)
    got = {}

    def wait(name, value):
        return gate(value, [got[other] for other in GATES.get(name, ())])

    places = [tuple(range(RING // 2)), tuple(range(RING // 2, RING))]
    kept, sent, sums, firsts, ends, blocks = {}, {}, {}, {}, {}, {}
    kept["d"], sent["d"], masked = down_call(table, pre_act, places[0], lengths, cotangent)
    kept["e"], sent["e"] = down_call(table, pre_act, places[1], masked=masked)
    split = pre_act.shape[1] // 8 * SPLIT

    def core(name):
        if name == "a":
            kept[name], sent[name], sent["x"] = up_call(
                table, layer_input, None, wait("ka", masked), pre_act, down_weight, 0, split
            )
        if name == "b":
            kept[name], sent[name] = up_call(
                table, layer_input, wait("kb", sent["x"]), masked, pre_act, down_weight,
                split, pre_act.shape[1] - split,
            )
        return inner_permute(wait(name + "0", sent[name]), core_route())

    def first(name):
        extra = [sent["e"]] if name == "d" else []
        other = gate(got[name + "0"], [got[o] for o in GATES.get(name + "1", ())] + extra)
        sums[name] = core_sum(kept[name], other)
        return ring_start(sums[name], 0)

    def second(name):
        return ring_pass(sums[name], 0, wait(name + "2", got[name + "1"]))

    def third(name):
        parts = {"d": "de", "a": "ab" if JOINT else "a"}.get(name, name)
        passed = wait(name + "3", [got[part + "2"] for part in parts])
        found = [ring_end(sums[part], got[part + "1"], two) for part, two in zip(parts, passed)]
        if name == "d":
            count = RING // len(parts)
            ends[name] = [
                lambda l, h=h: found[l // count][h](l % count) for h in range(HALVES)
            ]
        elif len(parts) > 1:
            ends[name] = [
                lambda l, h=h: jnp.stack([part[h](l) for part in found]) for h in range(HALVES)
            ]
        else:
            ends[name] = found[0]
        if RINGS[name]:
            return ring_start(once_reduced(ends[name]), 1)
        return direct(ends[name])

    def fourth(name):
        return ring_pass(once_reduced(ends[name]), 1, wait(name + "4", got[name + "3"]))

    def near(name):
        if RINGS[name]:
            last = wait(name + "5", got[name + "4"])
            blocks[name] = joined(ring_end(once_reduced(ends[name]), got[name + "3"], last))
        else:
            blocks[name] = direct_end(ends[name], wait(name + "5", got[name + "3"]))
        if FAR[name]:
            return neighbours(blocks[name])
        return across_replicas(blocks[name])[1:]

    def far(name):
        return opposite(wait(name + "6", got[name + "5"]))

    steps = [core, first, second, third, fourth, near, far]
    for item in ORDER:
        got[item] = steps[int(item[1])](item[0])
    groups = [
        held_blocks(blocks[name], got[name + "5"], got[name + "6"]) if FAR[name]
        else [blocks[name], *got[name + "5"]]
        for name in ("a" if JOINT else "ab") + "d"
    ]
    groups = [[x.reshape(-1, x.shape[-1]) for x in held] for held in groups]
    totals = sum_inner(jnp.stack([products_call(replica, held) for held in groups]))
    rows = layer_input.shape[1] // (CHIPS * CORES), pre_act.shape[1] // (CHIPS * CORES)
    return tuple(mix_call(replica, totals, rows, [groups[:-1], groups[-1:]]))


def solution(mesh):
    in_specs = (
        P(("inner", "rep"), None),
        P(("inner", "rep"), None),
        P(("inner", "rep"), None),
        P(),
        P(("inner", "rep")),
    )
    out_specs = (P("inner", None), P("inner", None))
    return jax.shard_map(
        on_device, mesh=mesh, in_specs=in_specs, out_specs=out_specs, check_vma=False
    )
```

```python
import functools
import math

import jax
import jax.numpy as jnp
from jax import lax
from jax.experimental import pallas as pl
from jax.experimental.pallas import tpu as pltpu
from jax.sharding import PartitionSpec as P

SEQ = 128
RING = 4
CORES = 2
CHIPS = RING * RING
HALVES = 2
LANES = 128
FF_BLOCK = 512
MIB = 1024 * 1024

EPSILON = 1e-06
SQRT_HALF = 0.7071067811865476
INV_ROOT_TWO_PI = 0.3989422804014327
EXP2_SCALE = -0.5 / math.log(2.0)
TERMS = 14
TERM_ROWS = 16


def device_of(y, z, core):
    return (y % RING * RING + z % RING) * CORES + core


def inner_route(move):
    route = []
    for y in range(RING):
        for z in range(RING):
            for core in range(CORES):
                route.append((device_of(y, z, core), device_of(*move(y, z, core))))
    return route


def ring_route(stage, step):
    return inner_route(
        lambda y, z, core: (y + step, z, core) if core == stage else (y, z + step, core)
    )


def core_route():
    return inner_route(lambda y, z, core: (y, z, 1 - core))


def inner_permute(block, route):
    return lax.ppermute(block, "inner", route)


def ring_start(piece, stage):
    return (
        inner_permute(jnp.stack([piece(2, 0), piece(1, 1)]), ring_route(stage, 1)),
        inner_permute(jnp.stack([piece(2, 1), piece(3, 0)]), ring_route(stage, -1)),
    )


def ring_pass(piece, stage, received):
    from_behind, from_ahead = received
    return (
        inner_permute(piece(1, 0) + from_behind[0], ring_route(stage, 1)),
        inner_permute(piece(3, 1) + from_ahead[0], ring_route(stage, -1)),
    )


def ring_end(piece, received, passed):
    from_behind, from_ahead = received
    return (
        lambda at: piece(0, 0)[at] + from_ahead[1][at] + passed[0][at],
        lambda at: piece(0, 1)[at] + from_behind[1][at] + passed[1][at],
    )


def once_reduced(halves):
    return lambda l, h: halves[h](l)


def joined(halves):
    return jnp.concatenate([half(...) for half in halves], axis=-2)


def direct(halves):
    return [
        inner_permute(jnp.stack([half(step) for half in halves]), ring_route(1, step))
        for step in range(1, RING)
    ]


def direct_end(halves, received):
    one, two, three = received
    return jnp.concatenate(
        [(half(0) + two[h]) + (one[h] + three[h]) for h, half in enumerate(halves)], axis=-2
    )


def core_sum(keep, other):
    return lambda k, h: keep[k, h] + other[k, h]


def gate(arrived, earlier=()):
    return lax.optimization_barrier((arrived, earlier))[0]


def destination_table():
    inner = lax.axis_index("inner")
    y, z, core = inner // (RING * CORES), inner // CORES % RING, inner % CORES
    k = lax.iota(jnp.int32, RING)[:, None]
    l = lax.iota(jnp.int32, RING)[None, :]

    def order(core_to):
        to_y = jnp.where(core_to == 0, y + k, y + l) % RING
        to_z = jnp.where(core_to == 0, z + l, z + k) % RING
        return (to_y * RING + to_z) * CORES + core_to

    return jnp.stack([order(core), order(1 - core)])


def write_masked(lengths_ref, cotangent_ref, masked_ref):
    columns = cotangent_ref.shape[1]
    for seq in range(cotangent_ref.shape[0] // SEQ):
        rows = slice(seq * SEQ, (seq + 1) * SEQ)
        valid = lax.broadcasted_iota(jnp.int32, (SEQ, columns), 0) < lengths_ref[seq]
        values = cotangent_ref[rows, :].astype(jnp.float32)
        masked_ref[rows, :] = jnp.where(valid, values, 0.0).astype(masked_ref.dtype)


def down_blocks(pre_refs, masked_ref, keep_ref, send_ref):
    rows = pre_refs[0].shape[1]
    for first in range(0, len(pre_refs), 2):
        columns = []
        for ref in pre_refs[first:first + 2]:
            value = ref[...].astype(jnp.float32)
            cdf = 0.5 + 0.5 * lax.erf(value * SQRT_HALF)
            columns.append((value * cdf).astype(jnp.bfloat16))
        product = lax.dot_general(
            jnp.concatenate(columns, axis=1), masked_ref[...], (((0,), (0,)), ((), ())),
            preferred_element_type=jnp.float32,
        )
        for index in range(2):
            which, place = divmod(first + index, len(pre_refs) // 2)
            out_ref = (keep_ref, send_ref)[which]
            part = product[index * rows:(index + 1) * rows]
            out_ref[0, :, place, :, :] = part.reshape(HALVES, rows // HALVES, part.shape[1])


def first_down_kernel(blocks_ref, lengths_ref, cotangent_ref, *refs):
    pre_refs, (keep_ref, send_ref, masked_ref) = refs[:-3], refs[-3:]

    @pl.when(pl.program_id(0) == 0)
    def _():
        write_masked(lengths_ref, cotangent_ref, masked_ref)

    down_blocks(pre_refs, masked_ref, keep_ref, send_ref)


def down_kernel(blocks_ref, masked_ref, *refs):
    down_blocks(refs[:-2], masked_ref, *refs[-2:])


def down_call(table, pre_act, places, lengths=None, cotangent=None, masked=None):
    is_first = masked is None
    tokens, width = (cotangent if is_first else masked).shape
    rows = pre_act.shape[1] // (CHIPS * CORES)

    def pre_spec(which, place):
        return pl.BlockSpec(
            (tokens, rows), lambda k, blocks_ref, *_: (0, blocks_ref[which * CHIPS + k * RING + place])
        )

    whole = pl.BlockSpec((tokens, width), lambda k, *_: (0, 0))
    out_block = pl.BlockSpec(
        (1, HALVES, len(places), rows // HALVES, width), lambda k, *_: (k, 0, 0, 0, 0)
    )
    out_shape = [
        jax.ShapeDtypeStruct((RING, HALVES, len(places), rows // HALVES, width), jnp.float32)
    ] * 2
    prefetch, wholes, extra = [table.reshape(-1)], [masked], []
    if is_first:
        prefetch, wholes, extra = prefetch + [lengths], [cotangent], [whole]
        out_shape = out_shape + [jax.ShapeDtypeStruct((tokens, width), jnp.bfloat16)]
    count = 2 * len(places)
    return pl.pallas_call(
        first_down_kernel if is_first else down_kernel,
        grid_spec=pltpu.PrefetchScalarGridSpec(
            num_scalar_prefetch=len(prefetch),
            grid=(RING,),
            in_specs=[whole] * len(wholes)
            + [pre_spec(which, place) for which in range(2) for place in places],
            out_specs=[out_block, out_block] + extra,
        ),
        out_shape=out_shape,
        compiler_params=pltpu.CompilerParams(vmem_limit_bytes=60 * MIB),
        cost_estimate=pl.CostEstimate(
            flops=2 * tokens * width * rows * RING * count,
            bytes_accessed=4 * tokens * width + (2 * tokens + 4 * width) * rows * RING * count,
            transcendentals=0,
        ),
        name="down_partial",
    )(*prefetch, *wholes, *[pre_act] * count)


def up_columns(ordered_ref, masked_ref, pre_ref, weight_ref, keep_ref, send_ref):
    tokens, width = masked_ref.shape
    grads = []
    part = tokens // 4
    for first in range(0, tokens, part):
        rows = slice(first, first + part)
        hidden_grad = lax.dot_general(
            masked_ref[rows, :], weight_ref[...], (((1,), (1,)), ((), ())),
            preferred_element_type=jnp.float32,
        )
        value = pre_ref[rows, :].astype(jnp.float32)
        cdf = 0.5 + 0.5 * lax.erf(value * SQRT_HALF)
        density = jnp.exp2(value * value * EXP2_SCALE)
        derivative = cdf + value * density * INV_ROOT_TWO_PI
        grads.append((hidden_grad * derivative).astype(jnp.bfloat16))
    grad = jnp.concatenate(grads, axis=0)
    half = width // CORES
    keep_ref[...] = jnp.dot(ordered_ref[:half, :], grad, preferred_element_type=jnp.float32)
    send_ref[...] = jnp.dot(ordered_ref[half:, :], grad, preferred_element_type=jnp.float32)


def first_up_kernel(rows_ref, x_ref, masked_ref, pre_ref, weight_ref,
                    keep_ref, send_ref, ordered_ref, turned_ref):
    @pl.when(pl.program_id(0) == 0)
    def _():
        strip = x_ref.shape[1] // (CHIPS * CORES * HALVES)
        turned_ref[...] = x_ref[...].T
        for index in range(x_ref.shape[1] // strip):
            start = pl.multiple_of(rows_ref[index], strip)
            ordered_ref[index * strip:(index + 1) * strip, :] = turned_ref[pl.ds(start, strip), :]

    up_columns(ordered_ref, masked_ref, pre_ref, weight_ref, keep_ref, send_ref)


def up_kernel(rows_ref, ordered_ref, masked_ref, pre_ref, weight_ref, keep_ref, send_ref):
    up_columns(ordered_ref, masked_ref, pre_ref, weight_ref, keep_ref, send_ref)


def up_call(table, x, ordered, masked, pre_act, weight, start, count):
    is_first = ordered is None
    tokens, width = masked.shape
    strip = width // (CHIPS * CORES * HALVES)
    half = lax.iota(jnp.int32, HALVES)[None, None, :, None]
    strips = (table[:, :, None, :] * HALVES + half).reshape(-1) * strip
    at = start // FF_BLOCK
    turned = pl.BlockSpec((width, tokens), lambda j, *_: (0, 0))
    whole = pl.BlockSpec((tokens, width), lambda j, *_: (0, 0))
    out_block = pl.BlockSpec((width // CORES, FF_BLOCK), lambda j, *_: (0, j))
    out_shape = [jax.ShapeDtypeStruct((width // CORES, count), jnp.float32)] * 2
    if is_first:
        out_shape = out_shape + [jax.ShapeDtypeStruct((width, tokens), jnp.bfloat16)]
    keep, send, *ordered_out = pl.pallas_call(
        first_up_kernel if is_first else up_kernel,
        grid_spec=pltpu.PrefetchScalarGridSpec(
            num_scalar_prefetch=1,
            grid=(count // FF_BLOCK,),
            in_specs=[
                whole if is_first else turned,
                whole,
                pl.BlockSpec((tokens, FF_BLOCK), lambda j, *_: (0, at + j)),
                pl.BlockSpec((FF_BLOCK, width), lambda j, *_: (at + j, 0)),
            ],
            out_specs=[out_block, out_block] + [turned] * is_first,
            scratch_shapes=[pltpu.VMEM((width, tokens), jnp.bfloat16)] * is_first,
        ),
        out_shape=out_shape,
        compiler_params=pltpu.CompilerParams(vmem_limit_bytes=34 * MIB),
        cost_estimate=pl.CostEstimate(
            flops=12 * tokens * width * count,
            bytes_accessed=4 * tokens * width + 2 * tokens * count + 6 * width * count,
            transcendentals=2 * tokens * count,
        ),
        name="up_partial",
    )(strips, x if is_first else ordered, masked, pre_act, weight)
    shape = (RING, HALVES, RING, strip, count)
    return keep.reshape(shape), send.reshape(shape), *ordered_out


def replica_route(step):
    count = lax.axis_size("rep")
    return [(i, (i + step) % count) for i in range(count)]


def neighbours(block):
    return tuple(lax.ppermute(block, "rep", replica_route(step)) for step in (1, -1))


def opposite(received):
    from_behind, from_ahead = received
    half = from_behind.shape[0] // 2
    return (
        lax.ppermute(from_behind[:half], "rep", replica_route(1)),
        lax.ppermute(from_ahead[half:], "rep", replica_route(-1)),
    )


def held_blocks(block, received, far):
    return [block, received[1], jnp.concatenate(far, axis=0), received[0]]


def across_replicas(block):
    return [block] + [lax.ppermute(block, "rep", replica_route(-step)) for step in range(1, RING)]


def in_order(values, replica):
    once = [jnp.where(replica % 2 == 1, values[i - 1], values[i]) for i in range(4)]
    return [jnp.where(replica // 2 == 1, once[i - 2], once[i]) for i in range(4)]


def products_kernel(replica_ref, *refs):
    held, out_ref = refs[:-1], refs[-1]
    replica = replica_ref[0]
    rows, columns = held[0].shape[-2:]

    def add_rows(index, totals):
        at = pl.ds(pl.multiple_of(index * 8, 8), 8)
        sums = [totals[i * 8:(i + 1) * 8, :] for i in range(TERMS)]
        for column in range(0, columns, LANES):
            a, d, b, e = in_order(
                [ref[at, column:column + LANES] for ref in held], replica
            )
            terms = []
            for left, right in ((a, b), (d, e)):
                both = left + right
                terms += [left * left, right * right, left * right, both * both,
                          both * (left - right)]
            terms += [a * d, a * e, b * d, b * e]
            sums = [total + term for total, term in zip(sums, terms)]
        return jnp.concatenate(sums, axis=0)

    totals = lax.fori_loop(0, rows // 8, add_rows, jnp.zeros((TERMS * 8, LANES), jnp.float32))
    for i in range(TERMS):
        out_ref[i:i + 1, :] = jnp.sum(totals[i * 8:(i + 1) * 8, :], axis=0, keepdims=True)
    out_ref[TERMS:, :] = jnp.zeros((TERM_ROWS - TERMS, LANES), jnp.float32)


def products_call(replica, held):
    vmem = pl.BlockSpec(memory_space=pltpu.VMEM)
    return pl.pallas_call(
        products_kernel,
        in_specs=[pl.BlockSpec(memory_space=pltpu.SMEM)] + [vmem] * len(held),
        out_specs=vmem,
        out_shape=jax.ShapeDtypeStruct((TERM_ROWS, LANES), jnp.float32),
        compiler_params=pltpu.CompilerParams(vmem_limit_bytes=24 * MIB),
        cost_estimate=pl.CostEstimate(
            flops=TERMS * 2 * held[0].size, bytes_accessed=16 * held[0].size, transcendentals=0
        ),
        name="inner_products",
    )(replica, *held)


def sum_inner(values):
    values = values + inner_permute(values, core_route())
    for axis in (0, 1):
        others = [
            inner_permute(values, inner_route(
                lambda y, z, core: (y + step, z, core) if axis == 0 else (y, z + step, core)))
            for step in (1, 2, 3)
        ]
        values = (values + others[1]) + (others[0] + others[2])
    return values


def pair_coefs(first_sq, second_sq, cross, both_sq, difference):
    first_wide, second_wide = first_sq + EPSILON, second_sq + EPSILON
    first_coef = 1.0 - cross / (2.0 * first_wide)
    second_coef = 1.0 - cross / (2.0 * second_wide)
    plain = (first_coef * first_coef * first_sq + 2.0 * first_coef * second_coef * cross
             + second_coef * second_coef * second_sq)
    mean = 0.5 * (first_coef + second_coef)
    skew = 0.25 * (cross / first_wide) * (difference / second_wide)
    apart = first_sq + second_sq - 2.0 * cross
    opposite = mean * mean * both_sq + 2.0 * mean * skew * difference + skew * skew * apart
    square = jnp.where(both_sq < 0.25 * (first_sq + second_sq), opposite, plain)
    return first_coef, second_coef, square


def coefficients(t):
    a, b, left = pair_coefs(*t[0:5])
    d, e, right = pair_coefs(*t[5:10])
    cross = a * (d * t[10] + e * t[11]) + b * (d * t[12] + e * t[13])
    left_coef = 1.0 - cross / (2.0 * (left + EPSILON))
    right_coef = 1.0 - cross / (2.0 * (right + EPSILON))
    return left_coef * a, right_coef * d, left_coef * b, right_coef * e


def mix_kernel(counts, replica_ref, totals_ref, *refs):
    groups, outs = refs[:-len(counts)], refs[-len(counts):]
    replica = replica_ref[0]
    group = 0
    for count, out_ref in zip(counts, outs):
        totals = totals_ref[group]
        for index in range(1, count):
            totals = totals + totals_ref[group + index]
        totals = jnp.sum(totals, axis=1, keepdims=True)
        coefs = coefficients([totals[i:i + 1, :] for i in range(TERMS)])
        start = 0
        for index in range(group, group + count):
            held = groups[4 * index:4 * index + 4]
            rows, columns = out_ref.shape[0], held[0].shape[1]
            for first in range(0, held[0].shape[0], rows):
                values = in_order([ref[first:first + rows, :] for ref in held], replica)
                a, d, b, e = [value * coef for value, coef in zip(values, coefs)]
                out_ref[:, start:start + columns] = (a + b) + (d + e)
                start += columns
        group += count


def mix_call(replica, totals, rows, outs):
    vmem = pl.BlockSpec(memory_space=pltpu.VMEM)
    flat = [block for groups in outs for held in groups for block in held]
    shapes = [
        jax.ShapeDtypeStruct((count, sum(held[0].size for held in groups) // count), jnp.float32)
        for count, groups in zip(rows, outs)
    ]
    size = sum(shape.size for shape in shapes)
    return pl.pallas_call(
        functools.partial(mix_kernel, [len(groups) for groups in outs]),
        in_specs=[pl.BlockSpec(memory_space=pltpu.SMEM)] + [vmem] * (len(flat) + 1),
        out_specs=[vmem] * len(shapes),
        out_shape=shapes,
        compiler_params=pltpu.CompilerParams(vmem_limit_bytes=24 * MIB),
        cost_estimate=pl.CostEstimate(flops=7 * size, bytes_accessed=20 * size, transcendentals=0),
        name="combine",
    )(replica, totals, *flat)


ORDER = ['d0', 'd1', 'e0', 'e1', 'a0', 'd2', 'e2', 'a1', 'b0', 'a2', 'b1', 'a3', 'd3', 'd5', 'b2', 'a4', 'b3', 'a5', 'a6', 'b5']
GATES = {'a0': ('d1', 'e1'), 'kb': ('a0',), 'b5': ('a5', 'a3'), 'd2': ('e1',)}
RINGS = {'a': True, 'b': False, 'd': False}
SPLIT = 4
FAR = {'a': True, 'b': False, 'd': False}
JOINT = False


def on_device(layer_input, pre_act, cotangent, down_weight, lengths):
    table = destination_table()
    replica = lax.axis_index("rep").reshape(1)
    got = {}

    def wait(name, value):
        return gate(value, [got[other] for other in GATES.get(name, ())])

    places = [tuple(range(RING // 2)), tuple(range(RING // 2, RING))]
    kept, sent, sums, firsts, ends, blocks = {}, {}, {}, {}, {}, {}
    kept["d"], sent["d"], masked = down_call(table, pre_act, places[0], lengths, cotangent)
    kept["e"], sent["e"] = down_call(table, pre_act, places[1], masked=masked)
    split = pre_act.shape[1] // 8 * SPLIT

    def core(name):
        if name == "a":
            kept[name], sent[name], sent["x"] = up_call(
                table, layer_input, None, wait("ka", masked), pre_act, down_weight, 0, split
            )
        if name == "b":
            kept[name], sent[name] = up_call(
                table, layer_input, wait("kb", sent["x"]), masked, pre_act, down_weight,
                split, pre_act.shape[1] - split,
            )
        return inner_permute(wait(name + "0", sent[name]), core_route())

    def first(name):
        extra = [sent["e"]] if name == "d" else []
        other = gate(got[name + "0"], [got[o] for o in GATES.get(name + "1", ())] + extra)
        sums[name] = core_sum(kept[name], other)
        return ring_start(sums[name], 0)

    def second(name):
        return ring_pass(sums[name], 0, wait(name + "2", got[name + "1"]))

    def third(name):
        parts = {"d": "de", "a": "ab" if JOINT else "a"}.get(name, name)
        passed = wait(name + "3", [got[part + "2"] for part in parts])
        found = [ring_end(sums[part], got[part + "1"], two) for part, two in zip(parts, passed)]
        if name == "d":
            count = RING // len(parts)
            ends[name] = [
                lambda l, h=h: found[l // count][h](l % count) for h in range(HALVES)
            ]
        elif len(parts) > 1:
            ends[name] = [
                lambda l, h=h: jnp.stack([part[h](l) for part in found]) for h in range(HALVES)
            ]
        else:
            ends[name] = found[0]
        if RINGS[name]:
            return ring_start(once_reduced(ends[name]), 1)
        return direct(ends[name])

    def fourth(name):
        return ring_pass(once_reduced(ends[name]), 1, wait(name + "4", got[name + "3"]))

    def near(name):
        if RINGS[name]:
            last = wait(name + "5", got[name + "4"])
            blocks[name] = joined(ring_end(once_reduced(ends[name]), got[name + "3"], last))
        else:
            blocks[name] = direct_end(ends[name], wait(name + "5", got[name + "3"]))
        if FAR[name]:
            return neighbours(blocks[name])
        return across_replicas(blocks[name])[1:]

    def far(name):
        return opposite(wait(name + "6", got[name + "5"]))

    steps = [core, first, second, third, fourth, near, far]
    for item in ORDER:
        got[item] = steps[int(item[1])](item[0])
    groups = [
        held_blocks(blocks[name], got[name + "5"], got[name + "6"]) if FAR[name]
        else [blocks[name], *got[name + "5"]]
        for name in ("a" if JOINT else "ab") + "d"
    ]
    groups = [[x.reshape(-1, x.shape[-1]) for x in held] for held in groups]
    totals = sum_inner(jnp.stack([products_call(replica, held) for held in groups]))
    rows = layer_input.shape[1] // (CHIPS * CORES), pre_act.shape[1] // (CHIPS * CORES)
    return tuple(mix_call(replica, totals, rows, [groups[:-1], groups[-1:]]))


def solution(mesh):
    in_specs = (
        P(("inner", "rep"), None),
        P(("inner", "rep"), None),
        P(("inner", "rep"), None),
        P(),
        P(("inner", "rep")),
    )
    out_specs = (P("inner", None), P("inner", None))
    return jax.shard_map(
        on_device, mesh=mesh, in_specs=in_specs, out_specs=out_specs, check_vma=False
    )
```
